32 devices in a mesh: row: 4 (over z), col: 4 (over x, core), dp: 2 (over y).
Axes of the slice: x: 2, y: 2, z: 4, core: 2. Of those that a mesh axis runs over, the one named last changes fastest.
Arguments:
- tokens: bfloat16 [1024, 8192], P(('dp', 'row'), 'col'), may hold values from -6 to 6
- w_in: bfloat16 [8192, 14336], P('col', 'row'), may hold values from -0.0625 to 0.0625
- w_out: bfloat16 [14336, 8192], P('row', 'col'), may hold values from -0.046875 to 0.046875
- spike_gain: float32 [14336], P('row'), may hold values from 1 to 4
- cotangent: bfloat16 [1024, 8192], P(('dp', 'row'), 'col'), may hold values from -1.5 to 1.5
Outputs:
- output: bfloat16 [1024, 8192], P(('dp', 'row'), 'col')
- grad_tokens: bfloat16 [1024, 8192], P(('dp', 'row'), 'col')
- grad_w_in: bfloat16 [8192, 14336], P('col', 'row')
- grad_w_out: bfloat16 [14336, 8192], P('row', 'col')
The draws below stay inside these ranges and needn't reach their ends.
All inputs are finite; a program needn't handle non-finite values.
Results may differ from the reference program's by a relative error of at most 0.035.
Values may be sent and summed in bfloat16 or wider, within the bound.
No kernel may reach another device: no remote copies, remote signals or barrier semaphores. Data moves between devices by JAX's collectives and lax.ppermute only.
A program may use at most 192 MiB of HBM per device.

```python
import math
import jax
import jax.numpy as jnp
from jax import lax

D = 8192
FF = 14336
LEVELS = 4
TOKENS = 1024
N_ROW = 4
N_COL = 4
N_DP = 2


def steps_of(stream_key, dims, pieces, least, top_value):
    loudness, own = 1.0, jax.random.fold_in(stream_key, 6)
    for position, blocks in pieces:
        heights = jnp.exp(jax.random.uniform(jax.random.fold_in(own, position), (blocks,), jnp.float32, least / len(pieces), top_value / len(pieces)))
        loudness = loudness * jnp.repeat(heights, dims[position] // blocks).reshape([-1 if axis == position else 1 for axis in range(len(dims))])
    return loudness


def gaussian(rng, extent, spread, reach, cuts=(), held_as=jnp.bfloat16):
    drawn = jax.random.normal(rng, extent, jnp.float32) * spread
    if len(cuts) > 0:
        drawn = steps_of(rng, extent, cuts, -0.22, 0.18) * drawn
    return jnp.clip(drawn, min=-reach, max=reach).astype(held_as)


def setup_inputs(seed: int = 0) -> dict:
    splits = jax.random.split(jax.random.key(seed), 6)
    return {
        "tokens": gaussian(splits[0], (TOKENS, D), 1.0, 6.0, ((0, 8), (1, 4))),
        "w_in": gaussian(splits[1], (D, FF), D ** -0.5, 0.0625, ((0, 4), (1, 4))),
        "w_out": gaussian(splits[2], (FF, D), FF ** -0.5, 0.046875, ((0, 4), (1, 4))),
        "spike_gain": jnp.clip(jnp.exp(math.log(4.0) - 1.3862944 * jax.random.uniform(splits[3], (FF,), jnp.float32) ** steps_of(splits[3], (FF,), ((0, 4),), -0.2, 0.2)), 1.0, 4.0),
        "cotangent": gaussian(splits[4], (TOKENS, D), 0.25, 1.5, ((0, 8), (1, 4))),
    }


sharpness = 4.0


def rounded(value):
    return lax.optimization_barrier(value.astype(jnp.bfloat16)).astype(jnp.float32)


def spike_parts(potential, gain):
    scaled = potential * gain[None, :]
    total = jnp.zeros_like(scaled)
    slope = jnp.zeros_like(scaled)
    for level in range(LEVELS):
        sig = jax.nn.sigmoid(sharpness * (scaled - (level + 0.5)))
        total = total + sig
        slope = slope + sig * (1.0 - sig)
    return total, slope * (sharpness * gain[None, :])


def reference(tokens, w_in, w_out, spike_gain, cotangent):
    feat = D // N_COL
    hid = FF // N_ROW
    run = TOKENS // N_DP
    potential = jnp.zeros((TOKENS, FF), jnp.float32)
    for block in range(N_COL):
        part = jnp.dot(tokens[:, block * feat:(block + 1) * feat], w_in[block * feat:(block + 1) * feat, :], preferred_element_type=jnp.float32)
        potential = potential + rounded(part)
    total, slope = spike_parts(potential, spike_gain)
    spikes = total.astype(jnp.bfloat16)
    output = jnp.zeros((TOKENS, D), jnp.float32)
    for block in range(N_ROW):
        part = jnp.dot(spikes[:, block * hid:(block + 1) * hid], w_out[block * hid:(block + 1) * hid, :], preferred_element_type=jnp.float32)
        output = output + rounded(part)
    grad_spikes = jnp.zeros((TOKENS, FF), jnp.float32)
    for block in range(N_COL):
        part = jnp.dot(cotangent[:, block * feat:(block + 1) * feat], w_out[:, block * feat:(block + 1) * feat].T, preferred_element_type=jnp.float32)
        grad_spikes = grad_spikes + rounded(part)
    grad_potential = (grad_spikes * slope).astype(jnp.bfloat16)
    grad_tokens = jnp.zeros((TOKENS, D), jnp.float32)
    for block in range(N_ROW):
        part = jnp.dot(grad_potential[:, block * hid:(block + 1) * hid], w_in[:, block * hid:(block + 1) * hid].T, preferred_element_type=jnp.float32)
        grad_tokens = grad_tokens + rounded(part)
    grad_w_in = jnp.zeros((D, FF), jnp.float32)
    grad_w_out = jnp.zeros((FF, D), jnp.float32)
    for half in range(N_DP):
        lower = half * run
        upper = (half + 1) * run
        grad_w_in = grad_w_in + rounded(jnp.dot(tokens[lower:upper].T, grad_potential[lower:upper], preferred_element_type=jnp.float32))
        grad_w_out = grad_w_out + rounded(jnp.dot(spikes[lower:upper].T, cotangent[lower:upper], preferred_element_type=jnp.float32))
    return (output.astype(jnp.bfloat16), grad_tokens.astype(jnp.bfloat16), grad_w_in.astype(jnp.bfloat16), grad_w_out.astype(jnp.bfloat16))
```

```python
import jax
import jax.numpy as jnp
from jax import lax
from jax.sharding import PartitionSpec as P

LEVELS = 4


sharpness = 4.0


def spike_parts(potential, gain):
    scaled = potential * gain[None, :]
    total = jnp.zeros_like(scaled)
    slope = jnp.zeros_like(scaled)
    for level in range(LEVELS):
        sig = jax.nn.sigmoid(sharpness * (scaled - (level + 0.5)))
        total = total + sig
        slope = slope + sig * (1.0 - sig)
    return (total, slope * (sharpness * gain[None, :]))


def times_transposed(left, right):
    return lax.dot_general(
        left, right, (((1,), (1,)), ((), ())), preferred_element_type=jnp.float32
    )


def over_tokens(left, right):
    return lax.dot_general(
        left, right, (((0,), (0,)), ((), ())), preferred_element_type=jnp.float32
    )


def from_other_halves(value, n_dp):
    return [
        lax.ppermute(value, "dp", [(d, (d + k) % n_dp) for d in range(n_dp)])
        for k in range(1, n_dp)
    ]


def shards(n_dp, tokens, w_in, w_out, spike_gain, cotangent):
    def gathered(value, axis):
        return lax.all_gather(value, axis, axis=0, tiled=True)

    def scattered(value, axis):
        return lax.psum_scatter(
            value.astype(jnp.bfloat16), axis, scatter_dimension=0, tiled=True
        )

    tok_all = gathered(tokens, "row")
    potential = scattered(
        jnp.dot(tok_all, w_in, preferred_element_type=jnp.float32), "col"
    ).astype(jnp.float32)
    cot_all = gathered(cotangent, "row")
    grad_spikes = scattered(times_transposed(cot_all, w_out), "col").astype(jnp.float32)
    total, slope = spike_parts(potential, spike_gain)
    spikes = total.astype(jnp.bfloat16)
    spike_all = gathered(spikes, "col")
    output = scattered(
        jnp.dot(spike_all, w_out, preferred_element_type=jnp.float32), "row"
    )
    grad_potential = (grad_spikes * slope).astype(jnp.bfloat16)
    grad_all = gathered(grad_potential, "col")
    grad_tokens = scattered(times_transposed(grad_all, w_in), "row")

    def every_half(own, others):
        return jnp.concatenate([own] + others, axis=0)

    tok_every = every_half(tok_all, from_other_halves(tok_all, n_dp))
    cot_every = every_half(cot_all, from_other_halves(cot_all, n_dp))
    spike_every = every_half(
        spike_all, [gathered(part, "col") for part in from_other_halves(spikes, n_dp)]
    )
    grad_every = every_half(
        grad_all,
        [gathered(part, "col") for part in from_other_halves(grad_potential, n_dp)],
    )
    grad_w_out = over_tokens(spike_every, cot_every).astype(jnp.bfloat16)
    grad_w_in = over_tokens(tok_every, grad_every).astype(jnp.bfloat16)
    return (output, grad_tokens, grad_w_in, grad_w_out)


def solution(mesh):
    placed = (
        P(("dp", "row"), "col"),
        P("col", "row"),
        P("row", "col"),
        P("row"),
        P(("dp", "row"), "col"),
    )

    def program(*args):
        return shards(mesh.shape["dp"], *args)

    return jax.shard_map(
        program,
        mesh=mesh,
        in_specs=placed,
        out_specs=(
            P(("dp", "row"), "col"),
            P(("dp", "row"), "col"),
            P("col", "row"),
            P("row", "col"),
        ),
        check_vma=False,
    )
```

```python
import jax
import jax.numpy as jnp
from jax import lax
from jax.sharding import PartitionSpec as P

LEVELS = 4
CORES = 2
CHUNKS = 1


sharpness = 4.0


def spike_parts(potential, gain):
    scaled = potential * gain[None, :]
    total = jnp.zeros_like(scaled)
    slope = jnp.zeros_like(scaled)
    for level in range(LEVELS):
        sig = jax.nn.sigmoid(sharpness * (scaled - (level + 0.5)))
        total = total + sig
        slope = slope + sig * (1.0 - sig)
    return (total, slope * (sharpness * gain[None, :]))


def times(left, right):
    return jnp.dot(left, right, preferred_element_type=jnp.float32)


def times_transposed(left, right):
    return lax.dot_general(
        left, right, (((1,), (1,)), ((), ())), preferred_element_type=jnp.float32
    )


def over_tokens(left, right):
    return lax.dot_general(
        left, right, (((0,), (0,)), ((), ())), preferred_element_type=jnp.float32
    )


def stacked(blocks):
    return jnp.concatenate(blocks, axis=0) if len(blocks) > 1 else blocks[0]


class Ring:
    def __init__(self, n):
        self.n = n
        self.pairs = [(i, (i + 1) % n) for i in range(n)]

    def step(self, value):
        return lax.ppermute(value, "row", self.pairs)

    def slots(self, own):
        held = [own]
        for _ in range(self.n - 1):
            held.append(self.step(held[-1]))
        return held

    def summed(self, slot):
        if self.n == 1:
            return slot(0).astype(jnp.bfloat16)
        held = slot(1).astype(jnp.bfloat16)
        for s in range(2, self.n + 1):
            arrived = self.step(held).astype(jnp.float32)
            held = (arrived + slot(s % self.n)).astype(jnp.bfloat16)
        return held


class Columns:
    def __init__(self, n):
        self.chips = n // CORES
        self.core = lax.rem(lax.axis_index("col"), CORES)
        self.chip = lax.div(lax.axis_index("col"), CORES)
        self.swap = [(i, i ^ 1) for i in range(n)]
        self.ahead = [
            [(i, (i + CORES * k) % n) for i in range(n)] for k in range(self.chips)
        ]

    def sibling(self, value):
        return lax.ppermute(value, "col", self.swap)

    def shifted(self, value, k):
        return lax.ppermute(value, "col", self.ahead[k])

    def summed(self, partial):
        half = partial.shape[0] // CORES
        own = lax.dynamic_slice_in_dim(partial, self.core * half, half)
        theirs = lax.dynamic_slice_in_dim(partial, (1 - self.core) * half, half)
        both = own.astype(jnp.float32) + self.sibling(theirs).astype(jnp.float32)
        rows = half // self.chips

        def part(chip):
            return lax.dynamic_slice_in_dim(both, lax.rem(chip, self.chips) * rows, rows)

        total = part(self.chip)
        for k in range(1, self.chips):
            arrived = self.shifted(part(self.chip + k).astype(jnp.bfloat16), k)
            total = total + arrived.astype(jnp.float32)
        return total

    def in_order(self, held):
        if len(held) == 1:
            return held
        if len(held) == 2:
            first = self.chip == 0
            return [
                jnp.where(first, held[0], held[1]),
                jnp.where(first, held[1], held[0]),
            ]
        every = jnp.stack(held)
        return [
            lax.dynamic_index_in_dim(
                every,
                lax.rem(self.chip + (self.chips - j), self.chips),
                keepdims=False,
            )
            for j in range(self.chips)
        ]

    def gathered(self, part):
        held = [part] + [self.shifted(part, k) for k in range(1, self.chips)]
        beside = [self.sibling(value) for value in held]
        mine, other = stacked(self.in_order(held)), stacked(self.in_order(beside))
        first = self.core == 0
        return stacked([jnp.where(first, mine, other), jnp.where(first, other, mine)])


def from_other_halves(value, n_dp):
    return [
        lax.ppermute(value, "dp", [(d, (d + k) % n_dp) for d in range(n_dp)])
        for k in range(1, n_dp)
    ]


def shards(sizes, tokens, w_in, w_out, spike_gain, cotangent):
    n_row, n_col, n_dp = sizes["row"], sizes["col"], sizes["dp"]
    ring, columns = Ring(n_row), Columns(n_col)
    chunks = CHUNKS if n_row % CHUNKS == 0 else 1
    per = n_row // chunks
    rows = tokens.shape[0]

    def in_chunks(slots):
        return [stacked(slots[c * per : (c + 1) * per]) for c in range(chunks)]

    def slot_of(products):
        def slot(s):
            at = (s % per) * rows
            return products[s // per][at : at + rows]

        return slot

    tok_slots = ring.slots(tokens)
    cotangent, _ = lax.optimization_barrier((cotangent, tok_slots[-1]))
    tok, cot = in_chunks(tok_slots), in_chunks(ring.slots(cotangent))
    spikes, slopes, grads = [], [], []
    for part in tok:
        potential = columns.summed(times(part, w_in).astype(jnp.bfloat16))
        total, slope = spike_parts(potential, spike_gain)
        spikes.append(total.astype(jnp.bfloat16))
        slopes.append(slope)
    for part, slope in zip(cot, slopes):
        grad_spikes = columns.summed(times_transposed(part, w_out).astype(jnp.bfloat16))
        grads.append((grad_spikes * slope).astype(jnp.bfloat16))
    spike_all = [columns.gathered(part) for part in spikes]
    output = ring.summed(slot_of([times(part, w_out) for part in spike_all]))
    grad_all = [columns.gathered(part) for part in grads]
    grad_tokens = ring.summed(slot_of([times_transposed(part, w_in) for part in grad_all]))

    def every(own, parts, finish):
        return stacked(
            own
            + [finish(other) for part in parts for other in from_other_halves(part, n_dp)]
        )

    def as_is(value):
        return value

    tok_every = every(tok, tok, as_is)
    cot_every = every(cot, cot, as_is)
    spike_every = every(spike_all, spikes, columns.gathered)
    grad_every = every(grad_all, grads, columns.gathered)
    grad_w_out = over_tokens(spike_every, cot_every).astype(jnp.bfloat16)
    grad_w_in = over_tokens(tok_every, grad_every).astype(jnp.bfloat16)
    return (output, grad_tokens, grad_w_in, grad_w_out)


def solution(mesh):
    placed = (
        P(("dp", "row"), "col"),
        P("col", "row"),
        P("row", "col"),
        P("row"),
        P(("dp", "row"), "col"),
    )

    def program(*args):
        return shards(mesh.shape, *args)

    return jax.shard_map(
        program,
        mesh=mesh,
        in_specs=placed,
        out_specs=(
            P(("dp", "row"), "col"),
            P(("dp", "row"), "col"),
            P("col", "row"),
            P("row", "col"),
        ),
        check_vma=False,
    )
```

```python
import jax
import jax.numpy as jnp
from jax import lax
from jax.sharding import PartitionSpec as P

LEVELS = 4
CORES = 2
CHUNKS = 2


sharpness = 4.0


def spike_parts(potential, gain):
    scaled = potential * gain[None, :]
    total = jnp.zeros_like(scaled)
    slope = jnp.zeros_like(scaled)
    for level in range(LEVELS):
        sig = jax.nn.sigmoid(sharpness * (scaled - (level + 0.5)))
        total = total + sig
        slope = slope + sig * (1.0 - sig)
    return (total, slope * (sharpness * gain[None, :]))


def times(left, right):
    return jnp.dot(left, right, preferred_element_type=jnp.float32)


def times_transposed(left, right):
    return lax.dot_general(
        left, right, (((1,), (1,)), ((), ())), preferred_element_type=jnp.float32
    )


def over_tokens(left, right):
    return lax.dot_general(
        left, right, (((0,), (0,)), ((), ())), preferred_element_type=jnp.float32
    )


def stacked(blocks):
    return jnp.concatenate(blocks, axis=0) if len(blocks) > 1 else blocks[0]


def wide(value):
    return value.astype(jnp.float32)


def narrow(value):
    return value.astype(jnp.bfloat16)


class Order:
    def __init__(self):
        self.last = {}

    def after(self, lane, *values):
        if lane not in self.last:
            return values
        return lax.optimization_barrier((*values, self.last[lane]))[: len(values)]

    def send(self, lane, value, axis, pairs):
        (value,) = self.after(lane, value)
        arrived = lax.ppermute(value, axis, pairs)
        self.last[lane] = arrived
        return arrived

    def compute(self, step, *values):
        done = step(*self.after("compute", *values))
        self.last["compute"] = done
        return done


class Mesh:
    def __init__(self, sizes, order):
        self.n_row, self.n_col, self.n_dp = sizes["row"], sizes["col"], sizes["dp"]
        self.chips = self.n_col // CORES
        self.order = order
        self.parts = [c + CORES * k for c in range(CORES) for k in range(self.chips)]


    def to_own_order(self, block):
        me, rows = lax.axis_index("col"), block.shape[0] // self.n_col
        return stacked(
            [
                lax.dynamic_slice_in_dim(block, jnp.bitwise_xor(me, part) * rows, rows)
                for part in self.parts
            ]
        )

    def to_plain_order(self, block):
        me, rows = lax.axis_index("col"), block.shape[0] // self.n_col
        found = []
        for natural in range(self.n_col):
            part = jnp.bitwise_xor(me, natural)
            at = lax.rem(part, CORES) * self.chips + lax.div(part, CORES)
            found.append(lax.dynamic_slice_in_dim(block, at * rows, rows))
        return stacked(found)

    def around(self, value):
        pairs = [(i, (i + 1) % self.n_row) for i in range(self.n_row)]
        return self.order.send("row", value, "row", pairs)

    def sibling(self, value):
        return lax.ppermute(value, "col", [(i, i ^ 1) for i in range(self.n_col)])

    def chip(self, value, k):
        pairs = [(i, i ^ (CORES * k)) for i in range(self.n_col)]
        return self.order.send("chip", value, "col", pairs)

    def half(self, value):
        n = self.n_dp
        return [
            self.order.send("dp", value, "dp", [(d, (d + k) % n) for d in range(n)])
            for k in range(1, n)
        ]

    def over_chips(self, part):
        return [part] + [self.chip(part, k) for k in range(1, self.chips)]

    def ring(self, own):
        held = [own]
        for _ in range(self.n_row - 1):
            held.append(self.around(held[-1]))
        return held

    def ring_sum(self, slot):
        held = slot(1 % self.n_row)
        for s in range(2, self.n_row + 1):
            held = wide(self.around(narrow(held))) + slot(s % self.n_row)
        return held


def shards(sizes, tokens, w_in, w_out, spike_gain, cotangent):
    order = Order()
    mesh = Mesh(sizes, order)
    n_row, n_col, chips = mesh.n_row, mesh.n_col, mesh.chips
    chunks = CHUNKS if n_row % CHUNKS == 0 else 1
    per = n_row // chunks
    rows = tokens.shape[0]
    piece = rows // n_col
    each = range(chunks)

    def chunk_of(slots):
        return stacked(
            [s[i * piece : (i + 1) * piece] for i in range(n_col) for s in slots]
        )

    def slot_of(products):
        def slot(s):
            value, at = products[s // per], s % per
            return stacked(
                [
                    value[(i * per + at) * piece : (i * per + at + 1) * piece]
                    for i in range(n_col)
                ]
            )

        return slot

    part = per * piece

    def part_of(value, k):
        return value[k * part : (k + 1) * part]

    def swapped(partial):
        cut = partial.shape[0] // CORES
        return partial[:cut], mesh.sibling(partial[cut:])

    def chip_sums(own, theirs):
        return tuple(
            narrow(wide(part_of(own, k)) + wide(part_of(theirs, k)))
            for k in range(1, chips)
        )

    def whole(own, theirs, arrived):
        total = wide(part_of(own, 0)) + wide(part_of(theirs, 0))
        for value in arrived:
            total = total + wide(value)
        return total

    def exchange(sums):
        return [mesh.chip(value, k) for k, value in zip(range(1, chips), sums)]

    def gathered(held):
        return held + [mesh.sibling(value) for value in held]

    def project(values):
        return narrow(times(values, w_in))

    def project_back(values):
        return narrow(times_transposed(values, w_out))

    def fire(own, theirs, *arrived):
        total, slope = spike_parts(whole(own, theirs, arrived), spike_gain)
        return narrow(total), slope

    def slope_back(own, theirs, slope, *arrived):
        return narrow(whole(own, theirs, arrived) * slope)

    def expand(*values):
        return times(stacked(values), w_out)

    def expand_back(*values):
        return times_transposed(stacked(values), w_in)

    def weight_part(left, right):
        return narrow(over_tokens(left, right))

    def weight_sum(sofar, left, right):
        return narrow(wide(sofar) + wide(over_tokens(left, right)))

    tok_slots = mesh.ring(mesh.to_own_order(tokens))
    cot_slots = mesh.ring(mesh.to_own_order(cotangent))

    def in_chunk(slots, c):
        return slots[c * per : (c + 1) * per]

    def slots_over_dp(slots):
        return [mesh.half(s) for s in slots]

    tok = [chunk_of(in_chunk(tok_slots, c)) for c in each]
    cot = [chunk_of(in_chunk(cot_slots, c)) for c in each]
    tok_other = [mesh.half(s) for s in tok_slots[:per]]
    cot_other = [mesh.half(cot_slots[0])]

    spikes, slopes, spike_held, spike_half = [], [], [], []
    grad_swap = []
    for c in each:
        swap = swapped(order.compute(project, tok[c]))
        sums = order.compute(chip_sums, *swap)
        arrived = exchange(sums)
        if c == chunks - 1:
            grad_swap.append(swapped(order.compute(project_back, cot[0])))
        spike, slope = order.compute(fire, *swap, *arrived)
        spikes.append(spike)
        slopes.append(slope)
        spike_held.append(mesh.over_chips(spike))
        spike_half.append(mesh.half(spike))
        if c == 0:
            tok_other += [mesh.half(s) for s in tok_slots[per:]]
    cot_other += [mesh.half(s) for s in cot_slots[1:per]]
    spike_all = [gathered(held) for held in spike_held]

    outs, grads, grad_held, grad_half, grad_arrived = [], [], [], [], []
    grad_sums = [order.compute(chip_sums, *grad_swap[0])]
    grad_arrived.append(exchange(grad_sums[0]))
    outs.append(order.compute(expand, *spike_all[0]))
    for c in range(1, chunks):
        grad_swap.append(swapped(order.compute(project_back, cot[c])))
        grad_sums.append(order.compute(chip_sums, *grad_swap[c]))
        grad_arrived.append(exchange(grad_sums[c]))
    for c in each:
        grads.append(
            order.compute(slope_back, *grad_swap[c], slopes[c], *grad_arrived[c])
        )
        grad_held.append(mesh.over_chips(grads[c]))
        grad_half.append(mesh.half(grads[c]))
        if c + 1 < chunks:
            outs.append(order.compute(expand, *spike_all[c + 1]))
    cot_other += [mesh.half(s) for s in cot_slots[per:]]
    grad_all = [gathered(held) for held in grad_held]

    output = mesh.ring_sum(slot_of(outs))
    spike_own = stacked([stacked(values) for values in spike_all])
    cot_own = stacked(cot)
    weight_out = order.compute(weight_part, spike_own, cot_own)
    back = [order.compute(expand_back, *values) for values in grad_all]
    grad_tokens = mesh.ring_sum(slot_of(back))
    tok_own = stacked(tok)
    grad_own = stacked([stacked(values) for values in grad_all])
    weight_in = order.compute(weight_part, tok_own, grad_own)

    for h in range(mesh.n_dp - 1):
        spike_far = [gathered(mesh.over_chips(half[h])) for half in spike_half]
        far = stacked([stacked(values) for values in spike_far])
        cot_far = stacked([chunk_of([s[h] for s in in_chunk(cot_other, c)]) for c in each])
        weight_out = order.compute(weight_sum, weight_out, far, cot_far)
        grad_far = [gathered(mesh.over_chips(half[h])) for half in grad_half]
        far = stacked([stacked(values) for values in grad_far])
        tok_far = stacked([chunk_of([s[h] for s in in_chunk(tok_other, c)]) for c in each])
        weight_in = order.compute(weight_sum, weight_in, tok_far, far)

    return (
        narrow(mesh.to_plain_order(output)),
        narrow(mesh.to_plain_order(grad_tokens)),
        weight_in,
        weight_out,
    )


def solution(mesh):
    placed = (
        P(("dp", "row"), "col"),
        P("col", "row"),
        P("row", "col"),
        P("row"),
        P(("dp", "row"), "col"),
    )

    def program(*args):
        return shards(mesh.shape, *args)

    return jax.shard_map(
        program,
        mesh=mesh,
        in_specs=placed,
        out_specs=(
            P(("dp", "row"), "col"),
            P(("dp", "row"), "col"),
            P("col", "row"),
            P("row", "col"),
        ),
        check_vma=False,
    )
```

```python
import functools

import jax
import jax.numpy as jnp
from jax import lax
from jax.experimental import pallas as pl
from jax.experimental.pallas import tpu as pltpu
from jax.sharding import PartitionSpec as P

LEVELS = 4
CORES = 2
CHUNKS = 2
MIB = 1 << 20


sharpness = 4.0


def spike_parts(potential, gain):
    scaled = potential * gain[None, :]
    total = jnp.zeros_like(scaled)
    slope = jnp.zeros_like(scaled)
    for level in range(LEVELS):
        sig = jax.nn.sigmoid(sharpness * (scaled - (level + 0.5)))
        total = total + sig
        slope = slope + sig * (1.0 - sig)
    return (total, slope * (sharpness * gain[None, :]))


def wide(value):
    return value.astype(jnp.float32)


def narrow(value):
    return value.astype(jnp.bfloat16)


def tile_of(size, most):
    best = 128
    for tile in range(128, most + 1, 128):
        if size % tile == 0:
            best = tile
    return best


def product(left, right, contract):
    return lax.dot_general(
        left, right, (contract, ((), ())), preferred_element_type=jnp.float32
    )


def whole_spec(value):
    return pl.BlockSpec(value.shape, lambda j, me: (0, 0), pipeline_mode=pl.Buffered(1))


def place_slots(slots, held):
    at = 0
    for slot in slots:
        rows = slot.shape[0]
        held[at : at + rows, :] = slot[...]
        at += rows


def place_parts(me, order, parts, held, base=0):
    for part, value in zip(order, parts):
        rows = value.shape[0]
        at = base + jnp.bitwise_xor(me, part) * rows
        held[pl.ds(pl.multiple_of(at, rows), rows), :] = value[...]


def weight_spec(weight, tile, transposed):
    if transposed:
        return pl.BlockSpec((tile, weight.shape[1]), lambda j, me: (j, 0))
    return pl.BlockSpec((weight.shape[0], tile), lambda j, me: (0, j))


def estimate(rows, weight, out):
    return pl.CostEstimate(
        flops=2 * rows * weight.size,
        bytes_accessed=2 * weight.size + out,
        transcendentals=0,
    )


def project_kernel(order, contract, n_slots, me, *refs):
    slots, weight, outs = refs[:n_slots], refs[n_slots], refs[n_slots + 1 : -2]
    plain, held = refs[-2:]

    @pl.when(pl.program_id(0) == 0)
    def _():
        place_slots(slots, plain)
        rows = held.shape[0] // len(order)
        for at, part in enumerate(order):
            start = pl.multiple_of(jnp.bitwise_xor(me[0], part) * rows, rows)
            held[at * rows : (at + 1) * rows, :] = plain[pl.ds(start, rows), :]

    result = narrow(product(held[...], weight[...], contract))
    cut = result.shape[0] // CORES
    for core, out in enumerate(outs):
        out[...] = result[core * cut : (core + 1) * cut]


def project(me, order, slots, weight, transposed):
    rows = sum(s.shape[0] for s in slots)
    depth = slots[0].shape[1]
    width = weight.shape[0 if transposed else 1]
    tile = tile_of(width, 512)
    cut = rows // CORES
    contract = ((1,), (1,)) if transposed else ((1,), (0,))
    return pl.pallas_call(
        functools.partial(project_kernel, order, contract, len(slots)),
        grid_spec=pltpu.PrefetchScalarGridSpec(
            num_scalar_prefetch=1,
            grid=(width // tile,),
            in_specs=[whole_spec(s) for s in slots]
            + [weight_spec(weight, tile, transposed)],
            out_specs=[pl.BlockSpec((cut, tile), lambda j, me: (0, j))] * CORES,
            scratch_shapes=[pltpu.VMEM((rows, depth), jnp.bfloat16)] * 2,
        ),
        out_shape=[jax.ShapeDtypeStruct((cut, width), jnp.bfloat16)] * CORES,
        compiler_params=pltpu.CompilerParams(vmem_limit_bytes=20 * MIB),
        cost_estimate=estimate(rows, weight, 2 * rows * width),
    )(me, *slots, weight)


def expand_kernel(order, contract, me, *refs):
    n = len(order)
    parts, weight, outs, held = refs[:n], refs[n], refs[n + 1 : -1], refs[-1]

    @pl.when(pl.program_id(0) == 0)
    def _():
        place_parts(me[0], order, parts, held)

    result = narrow(product(held[...], weight[...], contract))
    rows = outs[0].shape[0]
    for s, out in enumerate(outs):
        out[...] = result[s * rows : (s + 1) * rows]


def expand(me, order, parts, n_slots, weight, transposed):
    rows = len(parts) * parts[0].shape[0]
    depth = parts[0].shape[1]
    width = weight.shape[0 if transposed else 1]
    tile = tile_of(width, 256)
    each = rows // n_slots
    contract = ((1,), (1,)) if transposed else ((1,), (0,))
    return pl.pallas_call(
        functools.partial(expand_kernel, order, contract),
        grid_spec=pltpu.PrefetchScalarGridSpec(
            num_scalar_prefetch=1,
            grid=(width // tile,),
            in_specs=[whole_spec(p) for p in parts]
            + [weight_spec(weight, tile, transposed)],
            out_specs=[pl.BlockSpec((each, tile), lambda j, me: (0, j))] * n_slots,
            scratch_shapes=[pltpu.VMEM((rows, depth), jnp.bfloat16)],
        ),
        out_shape=[jax.ShapeDtypeStruct((each, width), jnp.bfloat16)] * n_slots,
        compiler_params=pltpu.CompilerParams(vmem_limit_bytes=20 * MIB),
        cost_estimate=estimate(rows, weight, 2 * rows * width),
    )(me, *parts, weight)


def weight_kernel(order, parts_left, n_slots, n_parts, tile, has_sofar, me, *refs):
    slots, parts = refs[:n_slots], refs[n_slots : n_slots + n_parts]
    sofar = refs[n_slots + n_parts] if has_sofar else None
    out, held_slots, held_parts = refs[-3:]
    step = pl.program_id(0)

    @pl.when(step == 0)
    def _():
        place_slots(slots, held_slots)
        for at in range(0, n_parts, len(order)):
            group = parts[at : at + len(order)]
            place_parts(me[0], order, group, held_parts, at * group[0].shape[0])

    left, right = (held_parts, held_slots) if parts_left else (held_slots, held_parts)
    columns = left[:, pl.ds(pl.multiple_of(step * tile, tile), tile)]
    result = product(columns, right[...], ((0,), (0,)))
    if has_sofar:
        result = result + wide(sofar[...])
    out[...] = narrow(result)


def weight_product(me, order, slots, parts, parts_left, sofar=None):
    rows = sum(s.shape[0] for s in slots)
    slot_width, part_width = slots[0].shape[1], parts[0].shape[1]
    tall, width = (part_width, slot_width) if parts_left else (slot_width, part_width)
    tile = tile_of(tall, 256)
    block = pl.BlockSpec((tile, width), lambda j, me: (j, 0))
    more = [] if sofar is None else [sofar]
    return pl.pallas_call(
        functools.partial(
            weight_kernel, order, parts_left, len(slots), len(parts), tile, len(more) > 0
        ),
        grid_spec=pltpu.PrefetchScalarGridSpec(
            num_scalar_prefetch=1,
            grid=(tall // tile,),
            in_specs=[whole_spec(s) for s in slots]
            + [whole_spec(p) for p in parts]
            + [block] * len(more),
            out_specs=block,
            scratch_shapes=[
                pltpu.VMEM((rows, slot_width), jnp.bfloat16),
                pltpu.VMEM((rows, part_width), jnp.bfloat16),
            ],
        ),
        out_shape=jax.ShapeDtypeStruct((tall, width), jnp.bfloat16),
        compiler_params=pltpu.CompilerParams(vmem_limit_bytes=40 * MIB),
        cost_estimate=pl.CostEstimate(
            flops=2 * rows * tall * width,
            bytes_accessed=2 * (1 + len(more)) * tall * width,
            transcendentals=0,
        ),
    )(me, *slots, *parts, *more)


class Order:
    def __init__(self):
        self.last = {}

    def after(self, lane, *values):
        if lane not in self.last:
            return values
        return lax.optimization_barrier((*values, self.last[lane]))[: len(values)]

    def send(self, lane, value, axis, pairs):
        (value,) = self.after(lane, value)
        arrived = lax.ppermute(value, axis, pairs)
        self.last[lane] = arrived
        return arrived

    def compute(self, step, *values):
        done = step(*self.after("compute", *values))
        self.last["compute"] = done[0] if isinstance(done, (tuple, list)) else done
        return done


class Mesh:
    def __init__(self, sizes, order):
        self.n_row, self.n_col, self.n_dp = sizes["row"], sizes["col"], sizes["dp"]
        self.chips = self.n_col // CORES
        self.order = order
        self.parts = tuple(c + CORES * k for c in range(CORES) for k in range(self.chips))

    def around(self, value):
        pairs = [(i, (i + 1) % self.n_row) for i in range(self.n_row)]
        return self.order.send("row", value, "row", pairs)

    def sibling(self, value):
        return lax.ppermute(value, "col", [(i, i ^ 1) for i in range(self.n_col)])

    def chip(self, value, k):
        pairs = [(i, i ^ (CORES * k)) for i in range(self.n_col)]
        return self.order.send("chip", value, "col", pairs)

    def half(self, value):
        n = self.n_dp
        return [
            self.order.send("dp", value, "dp", [(d, (d + k) % n) for d in range(n)])
            for k in range(1, n)
        ]

    def over_chips(self, part):
        return [part] + [self.chip(part, k) for k in range(1, self.chips)]

    def ring(self, own):
        held = [own]
        for _ in range(self.n_row - 1):
            held.append(self.around(held[-1]))
        return held

    def ring_sum(self, slots):
        held = slots[1 % self.n_row]
        for s in range(2, self.n_row + 1):
            held = narrow(wide(self.around(held)) + wide(slots[s % self.n_row]))
        return held


def shards(sizes, tokens, w_in, w_out, spike_gain, cotangent):
    order = Order()
    mesh = Mesh(sizes, order)
    n_row, n_col, chips = mesh.n_row, mesh.n_col, mesh.chips
    chunks = CHUNKS if n_row % CHUNKS == 0 else 1
    per = n_row // chunks
    part = per * tokens.shape[0] // n_col
    each = range(chunks)
    me = lax.axis_index("col").astype(jnp.int32).reshape(1)

    def part_of(value, k):
        return value[k * part : (k + 1) * part]

    def swapped(own, for_sibling):
        return own, mesh.sibling(for_sibling)

    def chip_sums(own, theirs):
        return tuple(
            narrow(wide(part_of(own, k)) + wide(part_of(theirs, k)))
            for k in range(1, chips)
        )

    def whole(own, theirs, arrived):
        total = wide(part_of(own, 0)) + wide(part_of(theirs, 0))
        for value in arrived:
            total = total + wide(value)
        return total

    def exchange(sums):
        return [mesh.chip(value, k) for k, value in zip(range(1, chips), sums)]

    def gathered(held):
        return held + [mesh.sibling(value) for value in held]

    def forward(*slots):
        return project(me, mesh.parts, slots, w_in, False)

    def backward(*slots):
        return project(me, mesh.parts, slots, w_out, True)

    def fire(own, theirs, *arrived):
        total, slope = spike_parts(whole(own, theirs, arrived), spike_gain)
        return narrow(total), slope

    def slope_back(own, theirs, slope, *arrived):
        return narrow(whole(own, theirs, arrived) * slope)

    def expand_out(*parts):
        return expand(me, mesh.parts, parts, per, w_out, False)

    def expand_back(*parts):
        return expand(me, mesh.parts, parts, per, w_in, True)

    def flat(lists):
        return [value for values in lists for value in values]

    def weights(parts_left, slots, parts, sofar=None):
        n = len(slots)

        def step(*values):
            return weight_product(
                me, mesh.parts, values[:n], values[n:], parts_left, sofar
            )

        return order.compute(step, *slots, *parts)

    tok = mesh.ring(tokens)
    cot = mesh.ring(cotangent)

    def chunk(slots, c):
        return slots[c * per : (c + 1) * per]

    tok_other = [mesh.half(s) for s in tok[:per]]
    cot_other = [mesh.half(cot[0])]

    spikes, slopes, spike_held, spike_half = [], [], [], []
    grad_swap = []
    for c in each:
        swap = swapped(*order.compute(forward, *chunk(tok, c)))
        sums = order.compute(chip_sums, *swap)
        arrived = exchange(sums)
        if c == chunks - 1:
            grad_swap.append(swapped(*order.compute(backward, *chunk(cot, 0))))
        spike, slope = order.compute(fire, *swap, *arrived)
        spikes.append(spike)
        slopes.append(slope)
        spike_held.append(mesh.over_chips(spike))
        spike_half.append(mesh.half(spike))
        if c == 0:
            tok_other += [mesh.half(s) for s in tok[per:]]
    cot_other += [mesh.half(s) for s in cot[1:per]]
    spike_all = [gathered(held) for held in spike_held]

    outs, grads, grad_held, grad_half, grad_arrived = [], [], [], [], []
    grad_sums = [order.compute(chip_sums, *grad_swap[0])]
    grad_arrived.append(exchange(grad_sums[0]))
    outs += order.compute(expand_out, *spike_all[0])
    for c in range(1, chunks):
        grad_swap.append(swapped(*order.compute(backward, *chunk(cot, c))))
        grad_sums.append(order.compute(chip_sums, *grad_swap[c]))
        grad_arrived.append(exchange(grad_sums[c]))
    for c in each:
        grads.append(
            order.compute(slope_back, *grad_swap[c], slopes[c], *grad_arrived[c])
        )
        grad_held.append(mesh.over_chips(grads[c]))
        grad_half.append(mesh.half(grads[c]))
        if c + 1 < chunks:
            outs += order.compute(expand_out, *spike_all[c + 1])
    cot_other += [mesh.half(s) for s in cot[per:]]
    grad_all = [gathered(held) for held in grad_held]

    output = mesh.ring_sum(outs)
    weight_out = weights(True, cot, flat(spike_all))
    back = flat([order.compute(expand_back, *parts) for parts in grad_all])
    grad_tokens = mesh.ring_sum(back)
    weight_in = weights(False, tok, flat(grad_all))

    for h in range(mesh.n_dp - 1):
        far = flat([gathered(mesh.over_chips(half[h])) for half in spike_half])
        weight_out = weights(True, [s[h] for s in cot_other], far, weight_out)
        far = flat([gathered(mesh.over_chips(half[h])) for half in grad_half])
        weight_in = weights(False, [s[h] for s in tok_other], far, weight_in)

    return (output, grad_tokens, weight_in, weight_out)


def solution(mesh):
    placed = (
        P(("dp", "row"), "col"),
        P("col", "row"),
        P("row", "col"),
        P("row"),
        P(("dp", "row"), "col"),
    )

    def program(*args):
        return shards(mesh.shape, *args)

    return jax.shard_map(
        program,
        mesh=mesh,
        in_specs=placed,
        out_specs=(
            P(("dp", "row"), "col"),
            P(("dp", "row"), "col"),
            P("col", "row"),
            P("row", "col"),
        ),
        check_vma=False,
    )
```

```python
import functools

import jax
import jax.numpy as jnp
from jax import lax
from jax.experimental import pallas as pl
from jax.experimental.pallas import tpu as pltpu
from jax.sharding import PartitionSpec as P

LEVELS = 4
CORES = 2
CHUNKS = 2
VMEM_LIMIT = 56 << 20


sharpness = 4.0


def spike_parts(potential, gain):
    scaled = potential * gain[None, :]
    total = jnp.zeros_like(scaled)
    slope = jnp.zeros_like(scaled)
    for level in range(LEVELS):
        sig = jax.nn.sigmoid(sharpness * (scaled - (level + 0.5)))
        total = total + sig
        slope = slope + sig * (1.0 - sig)
    return (total, slope * (sharpness * gain[None, :]))


def wide(value):
    return value.astype(jnp.float32)


def narrow(value):
    return value.astype(jnp.bfloat16)


def tile_of(size, most):
    best = 128
    for tile in range(128, most + 1, 128):
        if size % tile == 0:
            best = tile
    return best


def product(left, right, contract):
    return lax.dot_general(
        left, right, (contract, ((), ())), preferred_element_type=jnp.float32
    )


HERE = pl.BlockSpec(memory_space=pl.ANY)
NO_COST = pl.CostEstimate(flops=0, bytes_accessed=0, transcendentals=0)
PARAMS = pltpu.CompilerParams(vmem_limit_bytes=VMEM_LIMIT)


def copy_all(pairs, sems):
    copies = [
        pltpu.make_async_copy(source, target, sems.at[i])
        for i, (source, target) in enumerate(pairs)
    ]
    for copy in copies:
        copy.start()
    for copy in copies:
        copy.wait()


def slot_places(slots, held):
    rows = slots[0].shape[0]
    return [(slot, held.at[pl.ds(i * rows, rows)]) for i, slot in enumerate(slots)]


def plain_rows(me, core, chip_away, rows, first):
    chip = jnp.bitwise_xor(lax.div(me, CORES), chip_away)
    return pl.ds(pl.multiple_of(first + (chip * CORES + core) * rows, rows), rows)


def gathered_places(me, rows, gathered, held):
    places, first = [], 0
    for value in gathered:
        for core in range(CORES):
            for k in range(value.shape[1] // rows):
                source = value.at[core, pl.ds(k * rows, rows)]
                places.append((source, held.at[plain_rows(me, core, k, rows, first)]))
        first += CORES * value.shape[1]
    return places


def far_places(me, chips, parts, held, first):
    places, rows = [], parts[0].shape[0]
    for i, part in enumerate(parts):
        chunk, at = divmod(i, CORES * chips)
        core = lax.rem(me + at // chips, CORES)
        start = first + chunk * CORES * chips * rows
        where = plain_rows(me, core, at % chips, rows, start)
        places.append((part, held.at[where]))
    return places


def weight_spec(weight, tile, transposed):
    if transposed:
        return pl.BlockSpec((tile, weight.shape[1]), lambda j, me: (j, 0))
    return pl.BlockSpec((weight.shape[0], tile), lambda j, me: (0, j))


def project_kernel(rows, contract, n_slots, me, *refs):
    slots, weight, out = refs[:n_slots], refs[n_slots], refs[n_slots + 1]
    held, sems = refs[-2:]

    @pl.when(pl.program_id(0) == 0)
    def _():
        height = slots[0].shape[0]
        chips = held.shape[0] // rows // CORES
        piece, places = min(rows, height), []
        for first in range(0, held.shape[0], piece):
            part, within = divmod(first, rows)
            away = jnp.bitwise_xor(lax.div(me[0], CORES), part // CORES)
            at = (part % CORES * chips + away) * rows + within
            source = slots[first // height].at[pl.ds(first % height, piece)]
            target = held.at[pl.ds(pl.multiple_of(at, piece), piece)]
            places.append((source, target))
        copy_all(places, sems)

    result = narrow(product(held[...], weight[...], contract))
    cut = result.shape[0] // CORES
    for core in range(CORES):
        out[core] = result[core * cut : (core + 1) * cut]


def project(me, rows, slots, weight, transposed):
    total = sum(s.shape[0] for s in slots)
    depth = slots[0].shape[1]
    width = weight.shape[0 if transposed else 1]
    tile = tile_of(width, 512)
    cut = total // CORES
    contract = ((1,), (1,)) if transposed else ((1,), (0,))
    return pl.pallas_call(
        functools.partial(project_kernel, rows, contract, len(slots)),
        grid_spec=pltpu.PrefetchScalarGridSpec(
            num_scalar_prefetch=1,
            grid=(width // tile,),
            in_specs=[HERE] * len(slots) + [weight_spec(weight, tile, transposed)],
            out_specs=pl.BlockSpec((CORES, cut, tile), lambda j, me: (0, 0, j)),
            scratch_shapes=[
                pltpu.VMEM((total, depth), jnp.bfloat16),
                pltpu.SemaphoreType.DMA((max(total // rows, len(slots)),)),
            ],
        ),
        out_shape=jax.ShapeDtypeStruct((CORES, cut, width), jnp.bfloat16),
        compiler_params=PARAMS,
        cost_estimate=NO_COST,
    )(me, *slots, weight)


def expand_kernel(rows, contract, me, gathered, weight, *refs):
    outs, held, sems = refs[:-2], refs[-2], refs[-1]

    @pl.when(pl.program_id(0) == 0)
    def _():
        copy_all(gathered_places(me[0], rows, [gathered], held), sems)

    result = narrow(product(held[...], weight[...], contract))
    each = outs[0].shape[0]
    for s, out in enumerate(outs):
        out[...] = result[s * each : (s + 1) * each]


def expand(me, rows, gathered, n_slots, weight, transposed):
    total = CORES * gathered.shape[1]
    depth = gathered.shape[2]
    width = weight.shape[0 if transposed else 1]
    tile = tile_of(width, 256)
    each = total // n_slots
    contract = ((1,), (1,)) if transposed else ((1,), (0,))
    return pl.pallas_call(
        functools.partial(expand_kernel, rows, contract),
        grid_spec=pltpu.PrefetchScalarGridSpec(
            num_scalar_prefetch=1,
            grid=(width // tile,),
            in_specs=[HERE, weight_spec(weight, tile, transposed)],
            out_specs=[pl.BlockSpec((each, tile), lambda j, me: (0, j))] * n_slots,
            scratch_shapes=[
                pltpu.VMEM((total, depth), jnp.bfloat16),
                pltpu.SemaphoreType.DMA((total // rows,)),
            ],
        ),
        out_shape=[jax.ShapeDtypeStruct((each, width), jnp.bfloat16)] * n_slots,
        compiler_params=PARAMS,
        cost_estimate=NO_COST,
    )(me, gathered, weight)


def weight_kernel(rows, chips, parts_left, counts, tile, me, *refs):
    n_slots, n_gathered, n_far = counts
    slots, gathered = refs[:n_slots], refs[n_slots : n_slots + n_gathered]
    far = refs[n_slots + n_gathered : n_slots + n_gathered + n_far]
    out, held_slots, held_parts, sems = refs[-4:]
    step = pl.program_id(0)

    @pl.when(step == 0)
    def _():
        places = slot_places(slots, held_slots)
        places += gathered_places(me[0], rows, gathered, held_parts)
        first = sum(CORES * value.shape[1] for value in gathered)
        places += far_places(me[0], chips, far, held_parts, first)
        copy_all(places, sems)

    left, right = (held_parts, held_slots) if parts_left else (held_slots, held_parts)
    columns = left[:, pl.ds(pl.multiple_of(step * tile, tile), tile)]
    out[...] = narrow(product(columns, right[...], ((0,), (0,))))


def weight_product(me, rows, chips, slots, gathered, far, parts_left):
    total = sum(s.shape[0] for s in slots)
    slot_width, part_width = slots[0].shape[1], far[0].shape[1]
    tall, width = (part_width, slot_width) if parts_left else (slot_width, part_width)
    tile = tile_of(tall, 256)
    counts = (len(slots), len(gathered), len(far))
    copies = len(slots) + len(gathered) * CORES * chips + len(far)
    return pl.pallas_call(
        functools.partial(weight_kernel, rows, chips, parts_left, counts, tile),
        grid_spec=pltpu.PrefetchScalarGridSpec(
            num_scalar_prefetch=1,
            grid=(tall // tile,),
            in_specs=[HERE] * sum(counts),
            out_specs=pl.BlockSpec((tile, width), lambda j, me: (j, 0)),
            scratch_shapes=[
                pltpu.VMEM((total, slot_width), jnp.bfloat16),
                pltpu.VMEM((total, part_width), jnp.bfloat16),
                pltpu.SemaphoreType.DMA((copies,)),
            ],
        ),
        out_shape=jax.ShapeDtypeStruct((tall, width), jnp.bfloat16),
        compiler_params=PARAMS,
        cost_estimate=NO_COST,
    )(me, *slots, *gathered, *far)


class Program:
    def __init__(self, token):
        self.token = token

    def placed(self, values):
        return lax.optimization_barrier((*values, self.token))[:-1]

    def passed(self, values):
        *values, self.token = lax.optimization_barrier((*values, self.token))
        return values

    def start(self, value, axis, pairs):
        (value,) = self.placed([value])
        return lax.ppermute(value, axis, pairs)

    def wait(self, moving):
        return self.passed([moving])[0]

    def compute(self, step, *values):
        done = step(*self.placed(values))
        if isinstance(done, (tuple, list)):
            return self.passed(done)
        return self.passed([done])[0]


def shards(sizes, tokens, w_in, w_out, spike_gain, cotangent):
    n_row, n_col, n_dp = sizes["row"], sizes["col"], sizes["dp"]
    chips = n_col // CORES
    chunks = CHUNKS if n_row % CHUNKS == 0 else 1
    per = n_row // chunks
    part = per * tokens.shape[0] // n_col
    me = lax.axis_index("col").astype(jnp.int32).reshape(1)
    run = Program(me)

    def row_start(value):
        return run.start(value, "row", [(i, (i + 1) % n_row) for i in range(n_row)])

    def core_start(value):
        return run.start(value, "col", [(i, i ^ 1) for i in range(n_col)])

    def cores_exchange(value):
        pairs = [list(range(i, i + CORES)) for i in range(0, n_col, CORES)]
        return lax.all_to_all(value, "col", 0, 0, axis_index_groups=pairs)

    def chip_start(values):
        return [
            run.start(value, "col", [(i, i ^ (CORES * k)) for i in range(n_col)])
            for k, value in zip(range(1, chips), values)
        ]

    def half_start(value):
        return [
            run.start(value, "dp", [(d, (d + k) % n_dp) for d in range(n_dp)])
            for k in range(1, n_dp)
        ]

    def wait_all(moving):
        return [run.wait(value) for value in moving]

    def forward(*slots):
        return project(me, part, slots, w_in, False)

    def backward(*slots):
        return project(me, part, slots, w_out, True)

    def expand_out(gathered):
        return expand(me, part, gathered, per, w_out, False)

    def expand_back(gathered):
        return expand(me, part, gathered, per, w_in, True)

    def part_sum(partial, k):
        rows = slice(k * part, (k + 1) * part)
        return sum(wide(partial[core, rows]) for core in range(CORES))

    def chip_sums(partial):
        return [narrow(part_sum(partial, k)) for k in range(1, chips)]

    def whole(partial, arrived):
        total = part_sum(partial, 0)
        for value in arrived:
            total = total + wide(value)
        return total

    def fire(partial, *arrived):
        total, slope = spike_parts(whole(partial, arrived), spike_gain)
        return narrow(total), slope

    def slope_back(partial, slope, *arrived):
        return narrow(whole(partial, arrived) * slope)

    def both_cores(*held):
        mine = jnp.concatenate(held, axis=0)
        return cores_exchange(jnp.stack([mine] * CORES))

    def ring_add(arrived, slot):
        return narrow(wide(arrived) + wide(slot))

    def weight_step(parts_left):
        def weights(*values):
            slots, gathered = values[:n_all], values[n_all : n_all + chunks]
            far_parts = values[n_all + chunks :]
            return weight_product(me, part, chips, slots, gathered, far_parts, parts_left)

        return weights

    n_all = n_row * n_dp
    tok, cot, outs, back, summed = [], [], [], [], []

    def row_lane():
        for own, slots in ((tokens, tok), (cotangent, cot)):
            slots.append(own)
            for _ in range(n_row - 1):
                moving = row_start(slots[-1])
                yield
                slots.append(run.wait(moving))
        for slots in (outs, back):
            held = slots[1 % n_row]
            for s in range(2, n_row + 1):
                moving = row_start(held)
                yield
                held = run.compute(ring_add, run.wait(moving), slots[s % n_row])
            summed.append(held)

    row = row_lane()

    def turn():
        next(row, None)

    def until(slots, count):
        while len(slots) < count:
            turn()

    first, second = list(range(per)), list(range(per, n_row))
    far = {}
    spikes, slopes, grads = [], [], []
    sources = {"tok": tok, "cot": cot, "spike": spikes, "grad": grads}

    def half_lane():
        queue = [("tok", s) for s in first]
        queue += [("spike", 0)] + [("tok", s) for s in second[:1]]
        queue += [("spike", c) for c in range(1, chunks)]
        queue += [("tok", s) for s in second[1:]]
        queue += [("grad", 0), ("cot", 0)] + [("grad", c) for c in range(1, chunks)]
        queue += [("cot", s) for s in range(1, n_row)]
        for kind, at in queue:
            moving = half_start(sources[kind][at])
            yield
            far[kind, at] = wait_all(moving)

    half = half_lane()

    def half_turn():
        next(half, None)

    def projected(step, slots):
        return run.compute(cores_exchange, run.compute(step, *slots))

    def spreading(value):
        return value, chip_start([value] * (chips - 1))

    def chunk(slots, c):
        return slots[c * per : (c + 1) * per]

    turn()
    half_turn()
    until(tok, per)
    partial = projected(forward, chunk(tok, 0))
    moving = chip_start(run.compute(chip_sums, partial))
    half_turn()
    until(tok, n_row - 1)
    spike, slope = run.compute(fire, partial, *wait_all(moving))
    spikes.append(spike)
    slopes.append(slope)
    gather = spreading(spike)
    half_turn()
    until(tok, n_row)

    grad_partials, grad_sums, spike_all = [], [], []

    def project_back(c):
        until(cot, (c + 1) * per)
        grad_partials.append(projected(backward, chunk(cot, c)))
        grad_sums.append(run.compute(chip_sums, grad_partials[c]))

    def gathered(value, moving):
        return run.compute(both_cores, value, *wait_all(moving))

    for c in range(1, chunks):
        partial = projected(forward, chunk(tok, c))
        sums = run.compute(chip_sums, partial)
        arrived = wait_all(gather[1])
        moving = chip_start(sums)
        spike_all.append(run.compute(both_cores, gather[0], *arrived))
        half_turn()
        if c == 1:
            project_back(0)
        spike, slope = run.compute(fire, partial, *wait_all(moving))
        spikes.append(spike)
        slopes.append(slope)
        gather = spreading(spike)
        half_turn()
        outs.extend(run.compute(expand_out, spike_all[c - 1]))
    if chunks == 1:
        project_back(0)
    until(cot, n_row - 1)
    arrived = wait_all(gather[1])
    grad_moving = chip_start(grad_sums[0])
    half_turn()
    spike_all.append(run.compute(both_cores, gather[0], *arrived))
    outs.extend(run.compute(expand_out, spike_all[chunks - 1]))
    until(cot, n_row)

    grad_all = []
    for c in range(chunks):
        grad = run.compute(
            slope_back, grad_partials[c], slopes[c], *wait_all(grad_moving)
        )
        grads.append(grad)
        gather = spreading(grad)
        half_turn()
        if c + 1 < chunks:
            project_back(c + 1)
        else:
            turn()
        arrived = wait_all(gather[1])
        if c + 1 < chunks:
            grad_moving = chip_start(grad_sums[c + 1])
            turn()
        else:
            far_moving = chip_start(far["spike", 0][:1] * (chips - 1))
        half_turn()
        grad_all.append(run.compute(both_cores, gather[0], *arrived))
        back.extend(run.compute(expand_back, grad_all[c]))
    turn()

    todo = [
        (kind, c, h)
        for kind in ("spike", "grad")
        for h in range(n_dp - 1)
        for c in range(chunks)
    ]
    spread = {"spike": [], "grad": []}
    waiting = None

    def settle():
        if waiting is not None:
            kind, held, others = waiting
            spread[kind].extend(held + wait_all(others))

    def every(kind, slots):
        return slots + [far[kind, s][h] for h in range(n_dp - 1) for s in range(n_row)]

    for i, (kind, c, h) in enumerate(todo):
        own = far[kind, c][h]
        arrived = wait_all(far_moving)
        beside = [core_start(value) for value in [own] + arrived]
        if i + 1 < len(todo):
            kind_next, c_next, h_next = todo[i + 1]
            while (kind_next, c_next) not in far:
                half_turn()
            far_moving = chip_start([far[kind_next, c_next][h_next]] * (chips - 1))
        half_turn()
        settle()
        waiting = (kind, [own] + arrived, beside)
        if i + 2 == len(todo):
            while ("cot", n_row - 1) not in far:
                half_turn()
            weight_out = run.compute(
                weight_step(True), *every("cot", cot), *spike_all, *spread["spike"]
            )
        turn()
    settle()
    while len(summed) < 2:
        turn()
    weight_in = run.compute(
        weight_step(False), *every("tok", tok), *grad_all, *spread["grad"]
    )
    return (summed[0], summed[1], weight_in, weight_out)


def solution(mesh):
    placed = (
        P(("dp", "row"), "col"),
        P("col", "row"),
        P("row", "col"),
        P("row"),
        P(("dp", "row"), "col"),
    )

    def program(*args):
        return shards(mesh.shape, *args)

    return jax.shard_map(
        program,
        mesh=mesh,
        in_specs=placed,
        out_specs=(
            P(("dp", "row"), "col"),
            P(("dp", "row"), "col"),
            P("col", "row"),
            P("row", "col"),
        ),
        check_vma=False,
    )
```

```python
import functools

import jax
import jax.numpy as jnp
from jax import lax
from jax.experimental import pallas as pl
from jax.experimental.pallas import tpu as pltpu
from jax.sharding import PartitionSpec as P

LEVELS = 4
CORES = 2
CHUNKS = 2
VMEM_LIMIT = 56 << 20


sharpness = 4.0


def spike_parts(potential, gain):
    scaled = potential * gain[None, :]
    total = jnp.zeros_like(scaled)
    slope = jnp.zeros_like(scaled)
    for level in range(LEVELS):
        sig = jax.nn.sigmoid(sharpness * (scaled - (level + 0.5)))
        total = total + sig
        slope = slope + sig * (1.0 - sig)
    return (total, slope * (sharpness * gain[None, :]))


def wide(value):
    return value.astype(jnp.float32)


def narrow(value):
    return value.astype(jnp.bfloat16)


def tile_of(size, most):
    best = 128
    for tile in range(128, most + 1, 128):
        if size % tile == 0:
            best = tile
    return best


def product(left, right, contract):
    return lax.dot_general(
        left, right, (contract, ((), ())), preferred_element_type=jnp.float32
    )


HERE = pl.BlockSpec(memory_space=pl.ANY)
NO_COST = pl.CostEstimate(flops=0, bytes_accessed=0, transcendentals=0)
PARAMS = pltpu.CompilerParams(vmem_limit_bytes=VMEM_LIMIT)


def copies_of(pairs, sems):
    return [
        pltpu.make_async_copy(source, target, sems.at[i])
        for i, (source, target) in enumerate(pairs)
    ]


def start_all(copies):
    for copy in copies:
        copy.start()


def finish_all(copies):
    for copy in copies:
        copy.wait()


def slot_places(slots, held):
    rows = slots[0].shape[0]
    return [(slot, held.at[pl.ds(i * rows, rows)]) for i, slot in enumerate(slots)]


def plain_rows(me, away_core, away_chip, rows, first):
    core = jnp.bitwise_xor(lax.rem(me, CORES), away_core)
    chip = jnp.bitwise_xor(lax.div(me, CORES), away_chip)
    return first + (chip * CORES + core) * rows


def gathered_places(me, chips, rows, parts, held):
    places = []
    for i, value in enumerate(parts):
        chunk, at = divmod(i, CORES * chips)
        first = chunk * CORES * chips * rows
        start = plain_rows(me, at // chips, at % chips, rows, first)
        places.append((value, held.at[pl.ds(pl.multiple_of(start, rows), rows)]))
    return places


def weight_copies(weight, tiles, sems, transposed):
    count, tile = tiles.shape[0], tiles.shape[1 if transposed else 2]
    copies = []
    for j in range(count):
        where = pl.ds(j * tile, tile)
        source = weight.at[where] if transposed else weight.at[:, where]
        copies.append(pltpu.make_async_copy(source, tiles.at[j], sems.at[j]))
    return copies


def tile_scratch(weight, tile, transposed):
    if transposed:
        count, shape = weight.shape[0] // tile, (tile, weight.shape[1])
    else:
        count, shape = weight.shape[1] // tile, (weight.shape[0], tile)
    return [
        pltpu.VMEM((count, *shape), jnp.bfloat16),
        pltpu.SemaphoreType.DMA((count,)),
    ]


def product_kernel(place, transposed, n_in, n_out, me, *refs):
    sources, weight = refs[:n_in], refs[n_in]
    outs = refs[n_in + 1 : n_in + 1 + n_out]
    held, sems, tiles, tile_sems = refs[n_in + 1 + n_out :]
    contract = ((1,), (1,)) if transposed else ((1,), (0,))
    copies = copies_of(place(me[0], sources, held), sems)
    start_all(copies)
    weights = weight_copies(weight, tiles, tile_sems, transposed)
    start_all(weights)
    finish_all(copies)
    tile = tiles.shape[1 if transposed else 2]
    for j, copy in enumerate(weights):
        copy.wait()
        result = narrow(product(held[...], tiles[j], contract))
        first = 0
        for out in outs:
            rows = out.shape[0]
            out[:, j * tile : (j + 1) * tile] = result[first : first + rows]
            first += rows


def product_call(me, place, sources, n_copies, weight, transposed, out_rows):
    depth = sources[0].shape[1]
    width = weight.shape[0 if transposed else 1]
    tile = tile_of(width, 512)
    vmem = pl.BlockSpec(memory_space=pltpu.VMEM)
    return pl.pallas_call(
        functools.partial(
            product_kernel, place, transposed, len(sources), len(out_rows)
        ),
        in_specs=[pl.BlockSpec(memory_space=pltpu.SMEM)] + [HERE] * (len(sources) + 1),
        out_specs=[vmem] * len(out_rows),
        scratch_shapes=[
            pltpu.VMEM((sum(out_rows), depth), jnp.bfloat16),
            pltpu.SemaphoreType.DMA((n_copies,)),
            *tile_scratch(weight, tile, transposed),
        ],
        out_shape=[jax.ShapeDtypeStruct((rows, width), jnp.bfloat16) for rows in out_rows],
        compiler_params=PARAMS,
        cost_estimate=NO_COST,
    )(me, *sources, weight)


def project(me, chips, rows, slots, weight, transposed):
    total = sum(s.shape[0] for s in slots)
    height = slots[0].shape[0]
    piece = min(rows, height)

    def place(me, slots, held):
        places = []
        for first in range(0, total, piece):
            part, within = divmod(first, rows)
            core = jnp.bitwise_xor(lax.rem(me, CORES), part % CORES)
            chip = jnp.bitwise_xor(lax.div(me, CORES), part // CORES)
            at = pl.multiple_of((core * chips + chip) * rows + within, piece)
            source = slots[first // height].at[pl.ds(first % height, piece)]
            places.append((source, held.at[pl.ds(at, piece)]))
        return places

    cut = total // CORES
    out_rows = [cut] * CORES
    copies = total // piece
    return product_call(me, place, slots, copies, weight, transposed, out_rows)


def expand(me, chips, rows, parts, n_slots, weight, transposed):
    def place(me, parts, held):
        return gathered_places(me, chips, rows, parts, held)

    out_rows = [CORES * chips * rows // n_slots] * n_slots
    return product_call(me, place, parts, len(parts), weight, transposed, out_rows)


def weight_kernel(rows, chips, parts_left, n_slots, n_parts, tile, me, *refs):
    slots, parts = refs[:n_slots], refs[n_slots : n_slots + n_parts]
    out, held_slots, held_parts, sems = refs[-4:]
    step = pl.program_id(0)

    @pl.when(step == 0)
    def _():
        places = slot_places(slots, held_slots)
        places += gathered_places(me[0], chips, rows, parts, held_parts)
        copies = copies_of(places, sems)
        start_all(copies)
        finish_all(copies)

    left, right = (held_parts, held_slots) if parts_left else (held_slots, held_parts)
    columns = left[:, pl.ds(pl.multiple_of(step * tile, tile), tile)]
    out[...] = narrow(product(columns, right[...], ((0,), (0,))))


def weight_product(me, rows, chips, slots, parts, parts_left):
    total = sum(s.shape[0] for s in slots)
    slot_width, part_width = slots[0].shape[1], parts[0].shape[1]
    tall, width = (part_width, slot_width) if parts_left else (slot_width, part_width)
    tile = tile_of(tall, 512)
    return pl.pallas_call(
        functools.partial(
            weight_kernel, rows, chips, parts_left, len(slots), len(parts), tile
        ),
        grid_spec=pltpu.PrefetchScalarGridSpec(
            num_scalar_prefetch=1,
            grid=(tall // tile,),
            in_specs=[HERE] * (len(slots) + len(parts)),
            out_specs=pl.BlockSpec((tile, width), lambda j, me: (j, 0)),
            scratch_shapes=[
                pltpu.VMEM((total, slot_width), jnp.bfloat16),
                pltpu.VMEM((total, part_width), jnp.bfloat16),
                pltpu.SemaphoreType.DMA((len(slots) + len(parts),)),
            ],
        ),
        out_shape=jax.ShapeDtypeStruct((tall, width), jnp.bfloat16),
        compiler_params=PARAMS,
        cost_estimate=NO_COST,
    )(me, *slots, *parts)


class Program:
    def __init__(self, token):
        self.token = token

    def placed(self, values):
        return lax.optimization_barrier((*values, self.token))[:-1]

    def passed(self, values):
        *values, self.token = lax.optimization_barrier((*values, self.token))
        return values

    def start(self, value, axis, pairs):
        (value,) = self.placed([value])
        return lax.ppermute(value, axis, pairs)

    def wait(self, moving):
        return self.passed([moving])[0]

    def compute(self, step, *values):
        leaves, tree = jax.tree.flatten(step(*self.placed(values)))
        return jax.tree.unflatten(tree, self.passed(leaves))


def shards(sizes, tokens, w_in, w_out, spike_gain, cotangent):
    n_row, n_col, n_dp = sizes["row"], sizes["col"], sizes["dp"]
    chips = n_col // CORES
    chunks = CHUNKS if n_row % CHUNKS == 0 else 1
    per = n_row // chunks
    part = per * tokens.shape[0] // n_col
    me = lax.axis_index("col").astype(jnp.int32).reshape(1)
    run = Program(me)

    def row_start(value):
        return run.start(value, "row", [(i, (i + 1) % n_row) for i in range(n_row)])

    def core_start(value):
        return run.start(value, "col", [(i, i ^ 1) for i in range(n_col)])

    def chip_start(values):
        return [
            run.start(value, "col", [(i, i ^ (CORES * k)) for i in range(n_col)])
            for k, value in zip(range(1, chips), values)
        ]

    def half_start(value):
        return [
            run.start(value, "dp", [(d, (d + k) % n_dp) for d in range(n_dp)])
            for k in range(1, n_dp)
        ]

    def wait_all(moving):
        return [run.wait(value) for value in moving]

    def in_one_step(step):
        def taken(*values):
            def otherwise(*values):
                made = jax.eval_shape(step, *values)
                return jax.tree.map(lambda v: jnp.zeros(v.shape, v.dtype), made)

            return lax.cond(me[0] < n_col, step, otherwise, *values)

        taken.__name__ = step.__name__
        return taken

    def swap(value):
        return lax.ppermute(value, "col", [(i, i ^ 1) for i in range(n_col)])

    def part_sum(own, theirs, k):
        rows = slice(k * part, (k + 1) * part)
        return wide(own[rows]) + wide(theirs[rows])

    def summed_over_cores(weight, transposed, slots):
        own, for_sibling = project(me, chips, part, slots, weight, transposed)
        theirs = swap(for_sibling)
        sums = [narrow(part_sum(own, theirs, k)) for k in range(1, chips)]
        return [own, theirs] + sums

    @in_one_step
    def forward(*slots):
        return summed_over_cores(w_in, False, slots)

    @in_one_step
    def backward(*slots):
        return summed_over_cores(w_out, True, slots)

    def gathered(mine):
        return [*mine] + [swap(value) for value in mine]

    @in_one_step
    def expand_out(*mine):
        parts = gathered(mine)
        return expand(me, chips, part, parts, per, w_out, False), parts

    @in_one_step
    def expand_back(*mine):
        parts = gathered(mine)
        return expand(me, chips, part, parts, per, w_in, True), parts

    def whole(own, theirs, arrived):
        total = part_sum(own, theirs, 0)
        for value in arrived:
            total = total + wide(value)
        return total

    def fire(own, theirs, *arrived):
        total, slope = spike_parts(whole(own, theirs, arrived), spike_gain)
        return narrow(total), slope

    def slope_back(slope, own, theirs, *arrived):
        return narrow(whole(own, theirs, arrived) * slope)

    def ring_add(arrived, slot):
        return narrow(wide(arrived) + wide(slot))

    def weight_step(parts_left):
        def weights(*values):
            slots, parts = values[:n_all], values[n_all:]
            return weight_product(me, part, chips, slots, parts, parts_left)

        return weights

    n_all = n_row * n_dp
    tok, cot, outs, back, summed = [], [], [], [], []

    def row_lane():
        for own, slots in ((tokens, tok), (cotangent, cot)):
            slots.append(own)
            for _ in range(n_row - 1):
                moving = row_start(slots[-1])
                yield
                slots.append(run.wait(moving))
        for slots in (outs, back):
            held = slots[1 % n_row]
            for s in range(2, n_row + 1):
                moving = row_start(held)
                yield
                held = run.compute(ring_add, run.wait(moving), slots[s % n_row])
            summed.append(held)

    row = row_lane()

    def turn():
        next(row, None)

    def until(slots, count):
        while len(slots) < count:
            turn()

    first, second = list(range(per)), list(range(per, n_row))
    far = {}
    spikes, slopes, grads = [], [], []
    sources = {"tok": tok, "cot": cot, "spike": spikes, "grad": grads}

    def half_lane():
        queue = [("tok", s) for s in first]
        queue += [("spike", 0)] + [("tok", s) for s in second[:1]]
        queue += [("spike", c) for c in range(1, chunks)]
        queue += [("tok", s) for s in second[1:]]
        queue += [("grad", 0), ("cot", 0)] + [("grad", c) for c in range(1, chunks)]
        queue += [("cot", s) for s in range(1, n_row)]
        for kind, at in queue:
            moving = half_start(sources[kind][at])
            yield
            far[kind, at] = wait_all(moving)

    half = half_lane()

    def half_turn():
        next(half, None)

    def spreading(value):
        return value, chip_start([value] * (chips - 1))

    def both_cores(mine):
        return [core_start(value) for value in mine]

    def chunk(slots, c):
        return slots[c * per : (c + 1) * per]

    turn()
    half_turn()
    until(tok, per)
    own, theirs, *sums = run.compute(forward, *chunk(tok, 0))
    moving = chip_start(sums)
    half_turn()
    until(tok, n_row - 1)
    spike, slope = run.compute(fire, own, theirs, *wait_all(moving))
    spikes.append(spike)
    slopes.append(slope)
    gather = spreading(spike)
    half_turn()
    until(tok, n_row)

    grad_partials, grad_sums, mine, spike_all = [], [], [], []

    def project_back(c):
        until(cot, (c + 1) * per)
        own, theirs, *sums = run.compute(backward, *chunk(cot, c))
        grad_partials.append((own, theirs))
        grad_sums.append(sums)

    def expanded(c):
        slots, parts = run.compute(expand_out, *mine[c])
        outs.extend(slots)
        spike_all.extend(parts)

    for c in range(1, chunks):
        own, theirs, *sums = run.compute(forward, *chunk(tok, c))
        mine.append([gather[0]] + wait_all(gather[1]))
        moving = chip_start(sums)
        half_turn()
        if c == 1:
            project_back(0)
        spike, slope = run.compute(fire, own, theirs, *wait_all(moving))
        spikes.append(spike)
        slopes.append(slope)
        gather = spreading(spike)
        half_turn()
        expanded(c - 1)
    if chunks == 1:
        project_back(0)
    until(cot, n_row - 1)
    mine.append([gather[0]] + wait_all(gather[1]))
    grad_moving = chip_start(grad_sums[0])
    half_turn()
    expanded(chunks - 1)
    until(cot, n_row)

    grad_all = []
    for c in range(chunks):
        grad = run.compute(
            slope_back, slopes[c], *grad_partials[c], *wait_all(grad_moving)
        )
        grads.append(grad)
        gather = spreading(grad)
        half_turn()
        if c + 1 < chunks:
            project_back(c + 1)
        else:
            turn()
        grad_mine = [gather[0]] + wait_all(gather[1])
        if c + 1 < chunks:
            grad_moving = chip_start(grad_sums[c + 1])
            turn()
        else:
            far_moving = chip_start(far["spike", 0][:1] * (chips - 1))
        half_turn()
        slots, parts = run.compute(expand_back, *grad_mine)
        back.extend(slots)
        grad_all.extend(parts)
    turn()

    todo = [
        (kind, c, h)
        for kind in ("spike", "grad")
        for h in range(n_dp - 1)
        for c in range(chunks)
    ]
    spread = {"spike": [], "grad": []}
    waiting = None

    def settle():
        if waiting is not None:
            kind, held, others = waiting
            spread[kind].extend(held + wait_all(others))

    def every(kind, slots):
        return slots + [far[kind, s][h] for h in range(n_dp - 1) for s in range(n_row)]

    for i, (kind, c, h) in enumerate(todo):
        held = [far[kind, c][h]] + wait_all(far_moving)
        others = both_cores(held)
        if i + 1 < len(todo):
            kind_next, c_next, h_next = todo[i + 1]
            while (kind_next, c_next) not in far:
                half_turn()
            far_moving = chip_start([far[kind_next, c_next][h_next]] * (chips - 1))
        half_turn()
        settle()
        waiting = (kind, held, others)
        if i + 2 == len(todo):
            while ("cot", n_row - 1) not in far:
                half_turn()
            weight_out = run.compute(
                weight_step(True), *every("cot", cot), *spike_all, *spread["spike"]
            )
        turn()
    settle()
    while len(summed) < 2:
        turn()
    weight_in = run.compute(
        weight_step(False), *every("tok", tok), *grad_all, *spread["grad"]
    )
    return (summed[0], summed[1], weight_in, weight_out)


def solution(mesh):
    placed = (
        P(("dp", "row"), "col"),
        P("col", "row"),
        P("row", "col"),
        P("row"),
        P(("dp", "row"), "col"),
    )

    def program(*args):
        return shards(mesh.shape, *args)

    return jax.shard_map(
        program,
        mesh=mesh,
        in_specs=placed,
        out_specs=(
            P(("dp", "row"), "col"),
            P(("dp", "row"), "col"),
            P("col", "row"),
            P("row", "col"),
        ),
        check_vma=False,
    )
```

```python
import functools

import jax
import jax.numpy as jnp
from jax import lax
from jax.experimental import pallas as pl
from jax.experimental.pallas import tpu as pltpu
from jax.sharding import PartitionSpec as P

LEVELS = 4
CORES = 2
CHUNKS = 2
MIB = 1 << 20


sharpness = 4.0


def spike_parts(potential, gain):
    scaled = potential * gain[None, :]
    total = jnp.zeros_like(scaled)
    slope = jnp.zeros_like(scaled)
    for level in range(LEVELS):
        sig = jax.nn.sigmoid(sharpness * (scaled - (level + 0.5)))
        total = total + sig
        slope = slope + sig * (1.0 - sig)
    return (total, slope * (sharpness * gain[None, :]))


def wide(value):
    return value.astype(jnp.float32)


def narrow(value):
    return value.astype(jnp.bfloat16)


def tile_of(size, most):
    best = 128
    for tile in range(128, most + 1, 128):
        if size % tile == 0:
            best = tile
    return best


def product(left, right, contract):
    return lax.dot_general(
        left, right, (contract, ((), ())), preferred_element_type=jnp.float32
    )


HERE = pl.BlockSpec(memory_space=pl.ANY)
NO_COST = pl.CostEstimate(flops=0, bytes_accessed=0, transcendentals=0)
FAST = pl.BlockSpec(memory_space=pltpu.VMEM)


def copies_of(pairs, sems):
    return [
        pltpu.make_async_copy(source, target, sems.at[i])
        for i, (source, target) in enumerate(pairs)
    ]


def start_all(copies):
    for copy in copies:
        copy.start()


def finish_all(copies):
    for copy in copies:
        copy.wait()


def slot_places(slots, held):
    rows = slots[0].shape[0]
    return [(slot, held.at[pl.ds(i * rows, rows)]) for i, slot in enumerate(slots)]


def plain_rows(me, away_core, away_chip, rows, first):
    core = jnp.bitwise_xor(lax.rem(me, CORES), away_core)
    chip = jnp.bitwise_xor(lax.div(me, CORES), away_chip)
    return first + (chip * CORES + core) * rows


def gathered_places(me, chips, rows, parts, held):
    places = []
    for i, value in enumerate(parts):
        chunk, at = divmod(i, CORES * chips)
        first = chunk * CORES * chips * rows
        start = plain_rows(me, at // chips, at % chips, rows, first)
        places.append((value, held.at[pl.ds(pl.multiple_of(start, rows), rows)]))
    return places


def load_kernel(source, target, sems):
    rows = source.shape[0] // sems.shape[0]
    places = [
        (source.at[pl.ds(i * rows, rows)], target.at[pl.ds(i * rows, rows)])
        for i in range(sems.shape[0])
    ]
    copies = copies_of(places, sems)
    start_all(copies)
    finish_all(copies)


def load(weight):
    return pl.pallas_call(
        load_kernel,
        in_specs=[pl.BlockSpec(memory_space=pltpu.HBM)],
        out_specs=FAST,
        out_shape=pltpu.VMEM(weight.shape, weight.dtype),
        scratch_shapes=[pltpu.SemaphoreType.DMA((8,))],
        compiler_params=pltpu.CompilerParams(vmem_limit_bytes=12 * MIB),
        cost_estimate=NO_COST,
    )(pltpu.with_memory_space_constraint(weight, pltpu.HBM))


def product_kernel(place, transposed, n_in, n_out, me, *refs):
    sources, weight = refs[:n_in], refs[n_in]
    outs = refs[n_in + 1 : n_in + 1 + n_out]
    held, sems = refs[n_in + 1 + n_out :]
    contract = ((1,), (1,)) if transposed else ((1,), (0,))
    copies = copies_of(place(me[0], sources, held), sems)
    start_all(copies)
    finish_all(copies)
    width = weight.shape[0 if transposed else 1]
    tile = tile_of(width, 512)
    for j in range(width // tile):
        where = slice(j * tile, (j + 1) * tile)
        columns = weight[where, :] if transposed else weight[:, where]
        result = narrow(product(held[...], columns, contract))
        first = 0
        for out in outs:
            rows = out.shape[0]
            out[:, where] = result[first : first + rows]
            first += rows


def product_call(me, place, sources, n_copies, weight, transposed, out_rows):
    depth = sources[0].shape[1]
    width = weight.shape[0 if transposed else 1]
    return pl.pallas_call(
        functools.partial(
            product_kernel, place, transposed, len(sources), len(out_rows)
        ),
        in_specs=[pl.BlockSpec(memory_space=pltpu.SMEM)]
        + [HERE] * len(sources)
        + [FAST],
        out_specs=[FAST] * len(out_rows),
        scratch_shapes=[
            pltpu.VMEM((sum(out_rows), depth), jnp.bfloat16),
            pltpu.SemaphoreType.DMA((n_copies,)),
        ],
        out_shape=[jax.ShapeDtypeStruct((rows, width), jnp.bfloat16) for rows in out_rows],
        compiler_params=pltpu.CompilerParams(vmem_limit_bytes=12 * MIB),
        cost_estimate=NO_COST,
    )(me, *sources, weight)


def project(me, chips, rows, slots, weight, transposed):
    total = sum(s.shape[0] for s in slots)
    height = slots[0].shape[0]
    piece = min(rows, height)

    def place(me, slots, held):
        places = []
        for first in range(0, total, piece):
            part, within = divmod(first, rows)
            core = jnp.bitwise_xor(lax.rem(me, CORES), part % CORES)
            chip = jnp.bitwise_xor(lax.div(me, CORES), part // CORES)
            at = pl.multiple_of((core * chips + chip) * rows + within, piece)
            source = slots[first // height].at[pl.ds(first % height, piece)]
            places.append((source, held.at[pl.ds(at, piece)]))
        return places

    cut = total // CORES
    out_rows = [cut] * CORES
    copies = total // piece
    return product_call(me, place, slots, copies, weight, transposed, out_rows)


def expand(me, chips, rows, parts, n_slots, weight, transposed):
    def place(me, parts, held):
        return gathered_places(me, chips, rows, parts, held)

    out_rows = [CORES * chips * rows // n_slots] * n_slots
    return product_call(me, place, parts, len(parts), weight, transposed, out_rows)


def weight_kernel(rows, chips, parts_left, n_slots, n_parts, tile, first, me, *refs):
    slots, parts = refs[:n_slots], refs[n_slots : n_slots + n_parts]
    out, held_slots, held_parts, sems = refs[-4:]
    step = pl.program_id(0) + first

    @pl.when(pl.program_id(0) == 0)
    def _():
        places = slot_places(slots, held_slots)
        places += gathered_places(me[0], chips, rows, parts, held_parts)
        copies = copies_of(places, sems)
        start_all(copies)
        finish_all(copies)

    left, right = (held_parts, held_slots) if parts_left else (held_slots, held_parts)
    columns = left[:, pl.ds(pl.multiple_of(step * tile, tile), tile)]
    out[...] = narrow(product(columns, right[...], ((0,), (0,))))


def weight_product(me, rows, chips, slots, parts, parts_left, span=(0, 1), into=()):
    total = sum(s.shape[0] for s in slots)
    slot_width, part_width = slots[0].shape[1], parts[0].shape[1]
    tall, width = (part_width, slot_width) if parts_left else (slot_width, part_width)
    tile = tile_of(tall, 512)
    share, shares = span
    first, last = (tall // tile * at // shares for at in (share, share + 1))
    n_in = len(slots) + len(parts) + len(into)
    return pl.pallas_call(
        functools.partial(
            weight_kernel, rows, chips, parts_left, len(slots), len(parts), tile, first
        ),
        grid_spec=pltpu.PrefetchScalarGridSpec(
            num_scalar_prefetch=1,
            grid=(last - first,),
            in_specs=[HERE] * n_in,
            out_specs=pl.BlockSpec((tile, width), lambda j, me: (j + first, 0)),
            scratch_shapes=[
                pltpu.VMEM((total, slot_width), jnp.bfloat16),
                pltpu.VMEM((total, part_width), jnp.bfloat16),
                pltpu.SemaphoreType.DMA((len(slots) + len(parts),)),
            ],
        ),
        out_shape=jax.ShapeDtypeStruct((tall, width), jnp.bfloat16),
        input_output_aliases={n_in: 0} if into else {},
        compiler_params=pltpu.CompilerParams(vmem_limit_bytes=40 * MIB),
        cost_estimate=NO_COST,
    )(me, *slots, *parts, *into)


class Program:
    def __init__(self, token):
        self.token = token

    def placed(self, values):
        return lax.optimization_barrier((*values, self.token))[:-1]

    def passed(self, values):
        *values, self.token = lax.optimization_barrier((*values, self.token))
        return values

    def start(self, value, axis, pairs):
        (value,) = self.placed([value])
        return lax.ppermute(value, axis, pairs)

    def wait(self, moving):
        return self.passed([moving])[0]

    def compute(self, step, *values):
        leaves, tree = jax.tree.flatten(step(*self.placed(values)))
        return jax.tree.unflatten(tree, self.passed(leaves))


def shards(sizes, tokens, w_in, w_out, spike_gain, cotangent):
    n_row, n_col, n_dp = sizes["row"], sizes["col"], sizes["dp"]
    chips = n_col // CORES
    chunks = CHUNKS if n_row % CHUNKS == 0 else 1
    per = n_row // chunks
    part = per * tokens.shape[0] // n_col
    me = lax.axis_index("col").astype(jnp.int32).reshape(1)
    run = Program(me)

    def row_start(value):
        return run.start(value, "row", [(i, (i + 1) % n_row) for i in range(n_row)])

    def core_start(value):
        return run.start(value, "col", [(i, i ^ 1) for i in range(n_col)])

    def chip_start(values):
        return [
            run.start(value, "col", [(i, i ^ (CORES * k)) for i in range(n_col)])
            for k, value in zip(range(1, chips), values)
        ]

    def half_start(value):
        return [
            run.start(value, "dp", [(d, (d + k) % n_dp) for d in range(n_dp)])
            for k in range(1, n_dp)
        ]

    def wait_all(moving):
        return [run.wait(value) for value in moving]

    def in_one_step(step):
        def taken(*values):
            def otherwise(*values):
                made = jax.eval_shape(step, *values)
                return jax.tree.map(lambda v: jnp.zeros(v.shape, v.dtype), made)

            return lax.cond(me[0] < n_col, step, otherwise, *values)

        taken.__name__ = step.__name__
        return taken

    def swap(value):
        return lax.ppermute(value, "col", [(i, i ^ 1) for i in range(n_col)])

    def part_sum(own, theirs, k):
        rows = slice(k * part, (k + 1) * part)
        return wide(own[rows]) + wide(theirs[rows])

    def forward(*slots):
        return project(me, chips, part, slots, w_in_here, False)

    def backward(*slots):
        return project(me, chips, part, slots, w_out_here, True)

    @in_one_step
    def chip_sums(own, for_sibling):
        theirs = swap(for_sibling)
        return [theirs] + [narrow(part_sum(own, theirs, k)) for k in range(1, chips)]

    def projected(step, slots):
        own, for_sibling = run.compute(step, *slots)
        return [own] + run.compute(chip_sums, own, for_sibling)

    @in_one_step
    def both_cores_now(*mine):
        return [swap(value) for value in mine]

    def expand_out(*parts):
        return expand(me, chips, part, parts, per, w_out_here, False)

    def expand_back(*parts):
        return expand(me, chips, part, parts, per, w_in_here, True)

    def spread_out(step, mine):
        parts = [*mine] + run.compute(both_cores_now, *mine)
        return run.compute(step, *parts), parts

    def whole(own, theirs, arrived):
        total = part_sum(own, theirs, 0)
        for value in arrived:
            total = total + wide(value)
        return total

    def fire(own, theirs, *arrived):
        total, slope = spike_parts(whole(own, theirs, arrived), spike_gain)
        return narrow(total), slope

    def slope_back(slope, own, theirs, *arrived):
        return narrow(whole(own, theirs, arrived) * slope)

    def ring_add(arrived, slot):
        return narrow(wide(arrived) + wide(slot))

    def weight_step(parts_left, share, shares):
        n_into = 1 if share > 0 else 0

        def weights(*values):
            into, values = values[:n_into], values[n_into:]
            slots, parts = values[:n_all], values[n_all:]
            span = (share, shares)
            return weight_product(me, part, chips, slots, parts, parts_left, span, into)

        return weights

    n_all = n_row * n_dp
    tok, cot, outs, back, summed = [], [], [], [], []

    def row_lane():
        for own, slots in ((tokens, tok), (cotangent, cot)):
            slots.append(own)
            for _ in range(n_row - 1):
                moving = row_start(slots[-1])
                yield
                slots.append(run.wait(moving))
        for slots in (outs, back):
            held = slots[1 % n_row]
            for s in range(2, n_row + 1):
                moving = row_start(held)
                yield
                held = run.compute(ring_add, run.wait(moving), slots[s % n_row])
            summed.append(held)

    row = row_lane()

    def turn():
        next(row, None)

    def until(slots, count):
        while len(slots) < count:
            turn()

    first, second = list(range(per)), list(range(per, n_row))
    far = {}
    spikes, slopes, grads = [], [], []
    sources = {"tok": tok, "cot": cot, "spike": spikes, "grad": grads}

    def half_lane():
        queue = [("tok", s) for s in first] + [("spike", 0)]
        queue += [("tok", s) for s in second[:-1]]
        queue += [("spike", c) for c in range(1, chunks)]
        queue += [("cot", s) for s in first[:1]] + [("grad", 0)]
        queue += [("cot", s) for s in first[1:]]
        queue += [("grad", c) for c in range(1, chunks)]
        queue += [("cot", s) for s in second] + [("tok", s) for s in second[-1:]]
        for kind, at in queue:
            moving = half_start(sources[kind][at])
            yield
            far[kind, at] = wait_all(moving)

    half = half_lane()

    def half_turn():
        next(half, None)

    def spreading(value):
        return value, chip_start([value] * (chips - 1))

    def both_cores(mine):
        return [core_start(value) for value in mine]

    def chunk(slots, c):
        return slots[c * per : (c + 1) * per]

    turn()
    half_turn()
    w_in_here = run.compute(load, w_in)
    until(tok, per)
    own, theirs, *sums = projected(forward, chunk(tok, 0))
    moving = chip_start(sums)
    half_turn()
    until(tok, n_row - 1)
    spike, slope = run.compute(fire, own, theirs, *wait_all(moving))
    spikes.append(spike)
    slopes.append(slope)
    gather = spreading(spike)
    half_turn()
    until(tok, n_row)

    grad_partials, grad_sums, mine, spike_all = [], [], [], []

    def project_back(c):
        until(cot, (c + 1) * per)
        own, theirs, *sums = projected(backward, chunk(cot, c))
        grad_partials.append((own, theirs))
        grad_sums.append(sums)

    def expanded(c):
        slots, parts = spread_out(expand_out, mine[c])
        outs.extend(slots)
        spike_all.extend(parts)

    for c in range(1, chunks):
        own, theirs, *sums = projected(forward, chunk(tok, c))
        mine.append([gather[0]] + wait_all(gather[1]))
        moving = chip_start(sums)
        half_turn()
        if c + 1 == chunks:
            w_out_here = run.compute(load, w_out)
            project_back(0)
        spike, slope = run.compute(fire, own, theirs, *wait_all(moving))
        spikes.append(spike)
        slopes.append(slope)
        gather = spreading(spike)
        half_turn()
        expanded(c - 1)
    if chunks == 1:
        w_out_here = run.compute(load, w_out)
        project_back(0)
    until(cot, n_row - 1)
    mine.append([gather[0]] + wait_all(gather[1]))
    grad_moving = chip_start(grad_sums[0])
    half_turn()
    expanded(chunks - 1)
    until(cot, n_row)

    grad_all = []
    for c in range(chunks):
        grad = run.compute(
            slope_back, slopes[c], *grad_partials[c], *wait_all(grad_moving)
        )
        grads.append(grad)
        gather = spreading(grad)
        half_turn()
        if c + 1 < chunks:
            project_back(c + 1)
        else:
            turn()
        grad_mine = [gather[0]] + wait_all(gather[1])
        if c + 1 < chunks:
            grad_moving = chip_start(grad_sums[c + 1])
            turn()
        else:
            far_moving = chip_start(far["spike", 0][:1] * (chips - 1))
        half_turn()
        if c == 0:
            w_in_here = run.compute(load, w_in)
        slots, parts = spread_out(expand_back, grad_mine)
        back.extend(slots)
        grad_all.extend(parts)
    turn()

    todo = [
        (kind, c, h)
        for kind in ("spike", "grad")
        for h in range(n_dp - 1)
        for c in range(chunks)
    ]
    spread = {"spike": [], "grad": []}
    waiting = None

    def settle():
        if waiting is not None:
            kind, held, others = waiting
            spread[kind].extend(held + wait_all(others))

    def every(kind, slots):
        return slots + [far[kind, s][h] for h in range(n_dp - 1) for s in range(n_row)]

    def gradient(parts_left, share, shares, *into):
        kind, slots, parts = (
            ("spike", every("cot", cot), spike_all)
            if parts_left
            else ("grad", every("tok", tok), grad_all)
        )
        step = weight_step(parts_left, share, shares)
        return run.compute(step, *into, *slots, *parts, *spread[kind])

    spikes_last = len(todo) // 2 - 1
    weight_out = None
    for i, (kind, c, h) in enumerate(todo):
        held = [far[kind, c][h]] + wait_all(far_moving)
        others = both_cores(held)
        if i + 1 < len(todo):
            kind_next, c_next, h_next = todo[i + 1]
            while (kind_next, c_next) not in far:
                half_turn()
            far_moving = chip_start([far[kind_next, c_next][h_next]] * (chips - 1))
        half_turn()
        settle()
        waiting = (kind, held, others)
        if i == spikes_last:
            settle()
            waiting = None
            while ("cot", n_row - 1) not in far:
                half_turn()
            weight_out = gradient(True, 0, 2)
        elif i == spikes_last + 1:
            weight_out = gradient(True, 1, 2, weight_out)
        turn()
    settle()
    while len(summed) < 2:
        turn()
    while ("tok", n_row - 1) not in far:
        half_turn()
    weight_in = gradient(False, 0, 1)
    return (summed[0], summed[1], weight_in, weight_out)


def solution(mesh):
    placed = (
        P(("dp", "row"), "col"),
        P("col", "row"),
        P("row", "col"),
        P("row"),
        P(("dp", "row"), "col"),
    )

    def program(*args):
        return shards(mesh.shape, *args)

    return jax.shard_map(
        program,
        mesh=mesh,
        in_specs=placed,
        out_specs=(
            P(("dp", "row"), "col"),
            P(("dp", "row"), "col"),
            P("col", "row"),
            P("row", "col"),
        ),
        check_vma=False,
    )
```

```python
import functools

import jax
import jax.numpy as jnp
from jax import lax
from jax.experimental import pallas as pl
from jax.experimental.pallas import tpu as pltpu
from jax.sharding import PartitionSpec as P

LEVELS = 4
CORES = 2
CHUNKS = 2
MIB = 1 << 20
AHEAD = 3
SPLIT = 4


sharpness = 4.0


def spike_parts(potential, gain):
    scaled = potential * gain[None, :]
    total = jnp.zeros_like(scaled)
    slope = jnp.zeros_like(scaled)
    for level in range(LEVELS):
        sig = jax.nn.sigmoid(sharpness * (scaled - (level + 0.5)))
        total = total + sig
        slope = slope + sig * (1.0 - sig)
    return (total, slope * (sharpness * gain[None, :]))


def wide(value):
    return value.astype(jnp.float32)


def narrow(value):
    return value.astype(jnp.bfloat16)


def tile_of(size, most):
    best = 128
    for tile in range(128, most + 1, 128):
        if size % tile == 0:
            best = tile
    return best


def product(left, right, contract):
    return lax.dot_general(
        left, right, (contract, ((), ())), preferred_element_type=jnp.float32
    )


HERE = pl.BlockSpec(memory_space=pl.ANY)
NO_COST = pl.CostEstimate(flops=0, bytes_accessed=0, transcendentals=0)
FAST = pl.BlockSpec(memory_space=pltpu.VMEM)


def copies_of(pairs, sems):
    return [
        pltpu.make_async_copy(source, target, sems.at[i])
        for i, (source, target) in enumerate(pairs)
    ]


def start_all(copies):
    for copy in copies:
        copy.start()


def finish_all(copies):
    for copy in copies:
        copy.wait()


def slot_places(slots, held):
    rows = slots[0].shape[0]
    return [(slot, held.at[pl.ds(i * rows, rows)]) for i, slot in enumerate(slots)]


def plain_rows(me, away_core, away_chip, rows, first):
    core = jnp.bitwise_xor(lax.rem(me, CORES), away_core)
    chip = jnp.bitwise_xor(lax.div(me, CORES), away_chip)
    return first + (chip * CORES + core) * rows


def gathered_places(me, chips, rows, parts, held):
    places = []
    for i, value in enumerate(parts):
        chunk, at = divmod(i, CORES * chips)
        first = chunk * CORES * chips * rows
        start = plain_rows(me, at // chips, at % chips, rows, first)
        places.append((value, held.at[pl.ds(pl.multiple_of(start, rows), rows)]))
    return places


def tile_copies(weight, tiles, sems, j, transposed):
    at, copies = j % AHEAD, []
    depth, width = tiles.shape[1:]
    rows = depth // SPLIT
    for i in range(SPLIT):
        part = pl.ds(i * rows, rows)
        if transposed:
            source = weight.at[pl.ds(j * depth + i * rows, rows)]
        else:
            source = weight.at[part, pl.ds(j * width, width)]
        copies.append(
            pltpu.make_async_copy(source, tiles.at[at, part], sems.at[at, i])
        )
    return copies


def tile_scratch(weight, tile, transposed):
    shape = (tile, weight.shape[1]) if transposed else (weight.shape[0], tile)
    return [
        pltpu.VMEM((AHEAD, *shape), jnp.bfloat16),
        pltpu.SemaphoreType.DMA((AHEAD, SPLIT)),
    ]


def product_kernel(place, transposed, n_in, n_out, me, *refs):
    sources, weight = refs[:n_in], refs[n_in]
    outs = refs[n_in + 1 : n_in + 1 + n_out]
    held, sems, tiles, tile_sems = refs[n_in + 1 + n_out :]
    contract = ((1,), (1,)) if transposed else ((1,), (0,))
    tile = tiles.shape[1 if transposed else 2]
    count = weight.shape[0 if transposed else 1] // tile
    copies = copies_of(place(me[0], sources, held), sems)
    start_all(copies)
    moving = [tile_copies(weight, tiles, tile_sems, j, transposed) for j in range(count)]
    for j in range(min(AHEAD - 1, count)):
        start_all(moving[j])
    finish_all(copies)
    for j in range(count):
        if j + AHEAD - 1 < count:
            start_all(moving[j + AHEAD - 1])
        finish_all(moving[j])
        where = slice(j * tile, (j + 1) * tile)
        result = narrow(product(held[...], tiles[j % AHEAD], contract))
        first = 0
        for out in outs:
            rows = out.shape[0]
            out[:, where] = result[first : first + rows]
            first += rows


def product_call(me, place, sources, n_copies, weight, transposed, out_rows):
    depth = sources[0].shape[1]
    width = weight.shape[0 if transposed else 1]
    return pl.pallas_call(
        functools.partial(
            product_kernel, place, transposed, len(sources), len(out_rows)
        ),
        in_specs=[pl.BlockSpec(memory_space=pltpu.SMEM)]
        + [HERE] * (len(sources) + 1),
        out_specs=[FAST] * len(out_rows),
        scratch_shapes=[
            pltpu.VMEM((sum(out_rows), depth), jnp.bfloat16),
            pltpu.SemaphoreType.DMA((n_copies,)),
            *tile_scratch(weight, tile_of(width, 512), transposed),
        ],
        out_shape=[jax.ShapeDtypeStruct((rows, width), jnp.bfloat16) for rows in out_rows],
        compiler_params=pltpu.CompilerParams(vmem_limit_bytes=16 * MIB),
        cost_estimate=NO_COST,
    )(me, *sources, pltpu.with_memory_space_constraint(weight, pltpu.HBM))


def project(me, chips, rows, slots, weight, transposed):
    total = sum(s.shape[0] for s in slots)
    height = slots[0].shape[0]
    piece = min(rows, height)

    def place(me, slots, held):
        places = []
        for first in range(0, total, piece):
            part, within = divmod(first, rows)
            core = jnp.bitwise_xor(lax.rem(me, CORES), part % CORES)
            chip = jnp.bitwise_xor(lax.div(me, CORES), part // CORES)
            at = pl.multiple_of((core * chips + chip) * rows + within, piece)
            source = slots[first // height].at[pl.ds(first % height, piece)]
            places.append((source, held.at[pl.ds(at, piece)]))
        return places

    cut = total // CORES
    out_rows = [cut] * CORES
    copies = total // piece
    return product_call(me, place, slots, copies, weight, transposed, out_rows)


def expand(me, chips, rows, parts, n_slots, weight, transposed):
    def place(me, parts, held):
        return gathered_places(me, chips, rows, parts, held)

    out_rows = [CORES * chips * rows // n_slots] * n_slots
    return product_call(me, place, parts, len(parts), weight, transposed, out_rows)


def weight_kernel(rows, chips, parts_left, n_slots, n_parts, tile, first, me, *refs):
    slots, parts = refs[:n_slots], refs[n_slots : n_slots + n_parts]
    out, held_slots, held_parts, sems = refs[-4:]
    step = pl.program_id(0) + first

    @pl.when(pl.program_id(0) == 0)
    def _():
        places = slot_places(slots, held_slots)
        places += gathered_places(me[0], chips, rows, parts, held_parts)
        copies = copies_of(places, sems)
        start_all(copies)
        finish_all(copies)

    left, right = (held_parts, held_slots) if parts_left else (held_slots, held_parts)
    columns = left[:, pl.ds(pl.multiple_of(step * tile, tile), tile)]
    out[...] = narrow(product(columns, right[...], ((0,), (0,))))


def weight_product(me, rows, chips, slots, parts, parts_left, span=(0, 1), into=()):
    total = sum(s.shape[0] for s in slots)
    slot_width, part_width = slots[0].shape[1], parts[0].shape[1]
    tall, width = (part_width, slot_width) if parts_left else (slot_width, part_width)
    tile = tile_of(tall, 512)
    share, shares = span
    first, last = (tall // tile * at // shares for at in (share, share + 1))
    n_in = len(slots) + len(parts) + len(into)
    return pl.pallas_call(
        functools.partial(
            weight_kernel, rows, chips, parts_left, len(slots), len(parts), tile, first
        ),
        grid_spec=pltpu.PrefetchScalarGridSpec(
            num_scalar_prefetch=1,
            grid=(last - first,),
            in_specs=[HERE] * n_in,
            out_specs=pl.BlockSpec((tile, width), lambda j, me: (j + first, 0)),
            scratch_shapes=[
                pltpu.VMEM((total, slot_width), jnp.bfloat16),
                pltpu.VMEM((total, part_width), jnp.bfloat16),
                pltpu.SemaphoreType.DMA((len(slots) + len(parts),)),
            ],
        ),
        out_shape=jax.ShapeDtypeStruct((tall, width), jnp.bfloat16),
        input_output_aliases={n_in: 0} if into else {},
        compiler_params=pltpu.CompilerParams(vmem_limit_bytes=40 * MIB),
        cost_estimate=NO_COST,
    )(me, *slots, *parts, *into)


class Program:
    def __init__(self, token):
        self.token = token

    def placed(self, values):
        return lax.optimization_barrier((*values, self.token))[:-1]

    def passed(self, values):
        *values, self.token = lax.optimization_barrier((*values, self.token))
        return values

    def start(self, value, axis, pairs):
        (value,) = self.placed([value])
        return lax.ppermute(value, axis, pairs)

    def wait(self, moving):
        return self.passed([moving])[0]

    def compute(self, step, *values):
        leaves, tree = jax.tree.flatten(step(*self.placed(values)))
        return jax.tree.unflatten(tree, self.passed(leaves))


def shards(sizes, tokens, w_in, w_out, spike_gain, cotangent):
    n_row, n_col, n_dp = sizes["row"], sizes["col"], sizes["dp"]
    chips = n_col // CORES
    chunks = CHUNKS if n_row % CHUNKS == 0 else 1
    per = n_row // chunks
    part = per * tokens.shape[0] // n_col
    me = lax.axis_index("col").astype(jnp.int32).reshape(1)
    run = Program(me)

    def row_start(value):
        return run.start(value, "row", [(i, (i + 1) % n_row) for i in range(n_row)])

    def core_start(value):
        return run.start(value, "col", [(i, i ^ 1) for i in range(n_col)])

    def chip_start(values):
        return [
            run.start(value, "col", [(i, i ^ (CORES * k)) for i in range(n_col)])
            for k, value in zip(range(1, chips), values)
        ]

    def half_start(value):
        return [
            run.start(value, "dp", [(d, (d + k) % n_dp) for d in range(n_dp)])
            for k in range(1, n_dp)
        ]

    def wait_all(moving):
        return [run.wait(value) for value in moving]

    def in_one_step(step):
        def taken(*values):
            def otherwise(*values):
                made = jax.eval_shape(step, *values)
                return jax.tree.map(lambda v: jnp.zeros(v.shape, v.dtype), made)

            return lax.cond(me[0] < n_col, step, otherwise, *values)

        taken.__name__ = step.__name__
        return taken

    def swap(value):
        return lax.ppermute(value, "col", [(i, i ^ 1) for i in range(n_col)])

    def part_sum(own, theirs, k):
        rows = slice(k * part, (k + 1) * part)
        return wide(own[rows]) + wide(theirs[rows])

    def forward(*slots):
        return project(me, chips, part, slots, w_in, False)

    def backward(*slots):
        return project(me, chips, part, slots, w_out, True)

    @in_one_step
    def chip_sums(own, for_sibling):
        theirs = swap(for_sibling)
        return [theirs] + [narrow(part_sum(own, theirs, k)) for k in range(1, chips)]

    def projected(step, slots):
        own, for_sibling = run.compute(step, *slots)
        return [own] + run.compute(chip_sums, own, for_sibling)

    @in_one_step
    def both_cores_now(*mine):
        return [swap(value) for value in mine]

    def expand_out(*parts):
        return expand(me, chips, part, parts, per, w_out, False)

    def expand_back(*parts):
        return expand(me, chips, part, parts, per, w_in, True)

    def spread_out(step, mine):
        parts = [*mine] + run.compute(both_cores_now, *mine)
        return run.compute(step, *parts), parts

    def whole(own, theirs, arrived):
        total = part_sum(own, theirs, 0)
        for value in arrived:
            total = total + wide(value)
        return total

    def fire(own, theirs, *arrived):
        total, slope = spike_parts(whole(own, theirs, arrived), spike_gain)
        return narrow(total), slope

    def slope_back(slope, own, theirs, *arrived):
        return narrow(whole(own, theirs, arrived) * slope)

    def ring_add(arrived, slot):
        return narrow(wide(arrived) + wide(slot))

    def weight_step(parts_left, share, shares):
        n_into = 1 if share > 0 else 0

        def weights(*values):
            into, values = values[:n_into], values[n_into:]
            slots, parts = values[:n_all], values[n_all:]
            span = (share, shares)
            return weight_product(me, part, chips, slots, parts, parts_left, span, into)

        return weights

    n_all = n_row * n_dp
    tok, cot, outs, back, summed = [], [], [], [], []

    def row_lane():
        for own, slots in ((tokens, tok), (cotangent, cot)):
            slots.append(own)
            for _ in range(n_row - 1):
                moving = row_start(slots[-1])
                yield
                slots.append(run.wait(moving))
        for slots in (outs, back):
            held = slots[1 % n_row]
            for s in range(2, n_row + 1):
                moving = row_start(held)
                yield
                held = run.compute(ring_add, run.wait(moving), slots[s % n_row])
            summed.append(held)

    row = row_lane()

    def turn():
        next(row, None)

    def until(slots, count):
        while len(slots) < count:
            turn()

    first, second = list(range(per)), list(range(per, n_row))
    far = {}
    spikes, slopes, grads = [], [], []
    sources = {"tok": tok, "cot": cot, "spike": spikes, "grad": grads}

    def half_lane():
        queue = [("tok", s) for s in first] + [("spike", 0)]
        queue += [("tok", s) for s in second[:-1]]
        queue += [("spike", c) for c in range(1, chunks)]
        queue += [("cot", s) for s in first[:1]] + [("grad", 0)]
        queue += [("cot", s) for s in first[1:]]
        queue += [("grad", c) for c in range(1, chunks)]
        queue += [("cot", s) for s in second] + [("tok", s) for s in second[-1:]]
        for kind, at in queue:
            moving = half_start(sources[kind][at])
            yield
            far[kind, at] = wait_all(moving)

    half = half_lane()

    def half_turn():
        next(half, None)

    def spreading(value):
        return value, chip_start([value] * (chips - 1))

    def both_cores(mine):
        return [core_start(value) for value in mine]

    def chunk(slots, c):
        return slots[c * per : (c + 1) * per]

    turn()
    half_turn()
    until(tok, per)
    own, theirs, *sums = projected(forward, chunk(tok, 0))
    moving = chip_start(sums)
    half_turn()
    until(tok, n_row - 1)
    spike, slope = run.compute(fire, own, theirs, *wait_all(moving))
    spikes.append(spike)
    slopes.append(slope)
    gather = spreading(spike)
    half_turn()
    until(tok, n_row)

    grad_partials, grad_sums, mine, spike_all = [], [], [], []

    def project_back(c):
        until(cot, (c + 1) * per)
        own, theirs, *sums = projected(backward, chunk(cot, c))
        grad_partials.append((own, theirs))
        grad_sums.append(sums)

    def expanded(c):
        slots, parts = spread_out(expand_out, mine[c])
        outs.extend(slots)
        spike_all.extend(parts)

    for c in range(1, chunks):
        own, theirs, *sums = projected(forward, chunk(tok, c))
        mine.append([gather[0]] + wait_all(gather[1]))
        moving = chip_start(sums)
        half_turn()
        if c + 1 == chunks:
            project_back(0)
        spike, slope = run.compute(fire, own, theirs, *wait_all(moving))
        spikes.append(spike)
        slopes.append(slope)
        gather = spreading(spike)
        half_turn()
        expanded(c - 1)
    if chunks == 1:
        project_back(0)
    until(cot, n_row - 1)
    mine.append([gather[0]] + wait_all(gather[1]))
    grad_moving = chip_start(grad_sums[0])
    expanded(chunks - 1)
    half_turn()
    until(cot, n_row)

    grad_all = []
    for c in range(chunks):
        grad = run.compute(
            slope_back, slopes[c], *grad_partials[c], *wait_all(grad_moving)
        )
        grads.append(grad)
        gather = spreading(grad)
        half_turn()
        if c + 1 < chunks:
            project_back(c + 1)
        else:
            turn()
        grad_mine = [gather[0]] + wait_all(gather[1])
        if c + 1 < chunks:
            grad_moving = chip_start(grad_sums[c + 1])
            turn()
        else:
            far_moving = chip_start(far["spike", 0][:1] * (chips - 1))
        half_turn()
        slots, parts = spread_out(expand_back, grad_mine)
        back.extend(slots)
        grad_all.extend(parts)

    todo = [
        (kind, c, h)
        for kind in ("spike", "grad")
        for h in range(n_dp - 1)
        for c in range(chunks)
    ]
    spread = {"spike": [], "grad": []}
    waiting = None

    def settle():
        if waiting is not None:
            kind, held, others = waiting
            spread[kind].extend(held + wait_all(others))

    def every(kind, slots):
        return slots + [far[kind, s][h] for h in range(n_dp - 1) for s in range(n_row)]

    def gradient(parts_left, share, shares, *into):
        kind, slots, parts = (
            ("spike", every("cot", cot), spike_all)
            if parts_left
            else ("grad", every("tok", tok), grad_all)
        )
        step = weight_step(parts_left, share, shares)
        return run.compute(step, *into, *slots, *parts, *spread[kind])

    spikes_last = len(todo) // 2 - 1
    weight_out = None
    for i, (kind, c, h) in enumerate(todo):
        held = [far[kind, c][h]] + wait_all(far_moving)
        others = both_cores(held)
        if i + 1 < len(todo):
            kind_next, c_next, h_next = todo[i + 1]
            while (kind_next, c_next) not in far:
                half_turn()
            far_moving = chip_start([far[kind_next, c_next][h_next]] * (chips - 1))
        settle()
        waiting = (kind, held, others)
        if i < spikes_last:
            turn()
            half_turn()
        elif i == spikes_last:
            settle()
            waiting = None
            while ("cot", n_row - 1) not in far:
                half_turn()
            weight_out = gradient(True, 0, 2)
        elif i == spikes_last + 1:
            turn()
            weight_out = gradient(True, 1, 2, weight_out)
        else:
            turn()
    settle()
    while len(summed) < 2:
        turn()
    while ("tok", n_row - 1) not in far:
        half_turn()
    weight_in = gradient(False, 0, 1)
    return (summed[0], summed[1], weight_in, weight_out)


def solution(mesh):
    placed = (
        P(("dp", "row"), "col"),
        P("col", "row"),
        P("row", "col"),
        P("row"),
        P(("dp", "row"), "col"),
    )

    def program(*args):
        return shards(mesh.shape, *args)

    return jax.shard_map(
        program,
        mesh=mesh,
        in_specs=placed,
        out_specs=(
            P(("dp", "row"), "col"),
            P(("dp", "row"), "col"),
            P("col", "row"),
            P("row", "col"),
        ),
        check_vma=False,
    )
```

```python
import functools

import jax
import jax.numpy as jnp
from jax import lax
from jax.experimental import pallas as pl
from jax.experimental.pallas import tpu as pltpu
from jax.sharding import PartitionSpec as P

LEVELS = 4
CORES = 2
CHUNKS = 2
MIB = 1 << 20
AHEAD = 4
SPLIT = 4


sharpness = 4.0


def spike_parts(potential, gain):
    scaled = potential * gain[None, :]
    total = jnp.zeros_like(scaled)
    slope = jnp.zeros_like(scaled)
    for level in range(LEVELS):
        sig = jax.nn.sigmoid(sharpness * (scaled - (level + 0.5)))
        total = total + sig
        slope = slope + sig * (1.0 - sig)
    return (total, slope * (sharpness * gain[None, :]))


def wide(value):
    return value.astype(jnp.float32)


def narrow(value):
    return value.astype(jnp.bfloat16)


def tile_of(size, most):
    best = 128
    for tile in range(128, most + 1, 128):
        if size % tile == 0:
            best = tile
    return best


def product(left, right, contract):
    return lax.dot_general(
        left, right, (contract, ((), ())), preferred_element_type=jnp.float32
    )


HERE = pl.BlockSpec(memory_space=pl.ANY)
NO_COST = pl.CostEstimate(flops=0, bytes_accessed=0, transcendentals=0)
FAST = pl.BlockSpec(memory_space=pltpu.VMEM)


def copies_of(pairs, sems):
    return [
        pltpu.make_async_copy(source, target, sems.at[i])
        for i, (source, target) in enumerate(pairs)
    ]


def start_all(copies):
    for copy in copies:
        copy.start()


def finish_all(copies):
    for copy in copies:
        copy.wait()


def slot_places(slots, held):
    rows = slots[0].shape[0]
    return [(slot, held.at[pl.ds(i * rows, rows)]) for i, slot in enumerate(slots)]


def plain_rows(me, away_core, away_chip, rows, first):
    core = jnp.bitwise_xor(lax.rem(me, CORES), away_core)
    chip = jnp.bitwise_xor(lax.div(me, CORES), away_chip)
    return first + (chip * CORES + core) * rows


def gathered_places(me, chips, rows, parts, held):
    places = []
    for i, value in enumerate(parts):
        chunk, at = divmod(i, CORES * chips)
        first = chunk * CORES * chips * rows
        start = plain_rows(me, at // chips, at % chips, rows, first)
        places.append((value, held.at[pl.ds(pl.multiple_of(start, rows), rows)]))
    return places


def tile_copies(weight, tiles, sems, j, transposed):
    at, copies = j % AHEAD, []
    depth, width = tiles.shape[1:]
    rows = depth // SPLIT
    for i in range(SPLIT):
        part = pl.ds(i * rows, rows)
        if transposed:
            source = weight.at[pl.ds(j * depth + i * rows, rows)]
        else:
            source = weight.at[part, pl.ds(j * width, width)]
        copies.append(
            pltpu.make_async_copy(source, tiles.at[at, part], sems.at[at, i])
        )
    return copies


def tile_scratch(weight, tile, transposed):
    shape = (tile, weight.shape[1]) if transposed else (weight.shape[0], tile)
    return [
        pltpu.VMEM((AHEAD, *shape), jnp.bfloat16),
        pltpu.SemaphoreType.DMA((AHEAD, SPLIT)),
    ]


def product_kernel(place, transposed, n_in, n_out, me, *refs):
    sources, weight = refs[:n_in], refs[n_in]
    outs = refs[n_in + 1 : n_in + 1 + n_out]
    held, sems, tiles, tile_sems = refs[n_in + 1 + n_out :]
    contract = ((1,), (1,)) if transposed else ((1,), (0,))
    tile = tiles.shape[1 if transposed else 2]
    count = weight.shape[0 if transposed else 1] // tile
    copies = copies_of(place(me[0], sources, held), sems)
    start_all(copies)
    moving = [tile_copies(weight, tiles, tile_sems, j, transposed) for j in range(count)]
    for j in range(min(AHEAD - 1, count)):
        start_all(moving[j])
    finish_all(copies)
    for j in range(count):
        if j + AHEAD - 1 < count:
            start_all(moving[j + AHEAD - 1])
        finish_all(moving[j])
        where = slice(j * tile, (j + 1) * tile)
        result = narrow(product(held[...], tiles[j % AHEAD], contract))
        first = 0
        for out in outs:
            rows = out.shape[0]
            out[:, where] = result[first : first + rows]
            first += rows


def product_call(me, place, sources, n_copies, weight, transposed, out_rows):
    depth = sources[0].shape[1]
    width = weight.shape[0 if transposed else 1]
    return pl.pallas_call(
        functools.partial(
            product_kernel, place, transposed, len(sources), len(out_rows)
        ),
        in_specs=[pl.BlockSpec(memory_space=pltpu.SMEM)]
        + [HERE] * (len(sources) + 1),
        out_specs=[FAST] * len(out_rows),
        scratch_shapes=[
            pltpu.VMEM((sum(out_rows), depth), jnp.bfloat16),
            pltpu.SemaphoreType.DMA((n_copies,)),
            *tile_scratch(weight, tile_of(width, min(MIB // depth, 512)), transposed),
        ],
        out_shape=[jax.ShapeDtypeStruct((rows, width), jnp.bfloat16) for rows in out_rows],
        compiler_params=pltpu.CompilerParams(vmem_limit_bytes=18 * MIB),
        cost_estimate=NO_COST,
    )(me, *sources, pltpu.with_memory_space_constraint(weight, pltpu.HBM))


def project(me, chips, rows, slots, weight, transposed):
    total = sum(s.shape[0] for s in slots)
    height = slots[0].shape[0]
    piece = min(rows, height)

    def place(me, slots, held):
        places = []
        for first in range(0, total, piece):
            part, within = divmod(first, rows)
            core = jnp.bitwise_xor(lax.rem(me, CORES), part % CORES)
            chip = jnp.bitwise_xor(lax.div(me, CORES), part // CORES)
            at = pl.multiple_of((core * chips + chip) * rows + within, piece)
            source = slots[first // height].at[pl.ds(first % height, piece)]
            places.append((source, held.at[pl.ds(at, piece)]))
        return places

    cut = total // CORES
    out_rows = [cut] * CORES
    copies = total // piece
    return product_call(me, place, slots, copies, weight, transposed, out_rows)


def expand(me, chips, rows, parts, n_slots, weight, transposed):
    def place(me, parts, held):
        return gathered_places(me, chips, rows, parts, held)

    out_rows = [CORES * chips * rows // n_slots] * n_slots
    return product_call(me, place, parts, len(parts), weight, transposed, out_rows)


def weight_kernel(rows, chips, parts_left, n_slots, n_parts, tile, first, me, *refs):
    slots, parts = refs[:n_slots], refs[n_slots : n_slots + n_parts]
    out, held_slots, held_parts, sems = refs[-4:]
    step = pl.program_id(0) + first

    @pl.when(pl.program_id(0) == 0)
    def _():
        places = slot_places(slots, held_slots)
        places += gathered_places(me[0], chips, rows, parts, held_parts)
        copies = copies_of(places, sems)
        start_all(copies)
        finish_all(copies)

    left, right = (held_parts, held_slots) if parts_left else (held_slots, held_parts)
    columns = left[:, pl.ds(pl.multiple_of(step * tile, tile), tile)]
    out[...] = narrow(product(columns, right[...], ((0,), (0,))))


def weight_product(me, rows, chips, slots, parts, parts_left, span=(0, 1), into=()):
    total = sum(s.shape[0] for s in slots)
    slot_width, part_width = slots[0].shape[1], parts[0].shape[1]
    tall, width = (part_width, slot_width) if parts_left else (slot_width, part_width)
    tile = tile_of(tall, 512)
    share, shares = span
    first, last = (tall // tile * at // shares for at in (share, share + 1))
    n_in = len(slots) + len(parts) + len(into)
    return pl.pallas_call(
        functools.partial(
            weight_kernel, rows, chips, parts_left, len(slots), len(parts), tile, first
        ),
        grid_spec=pltpu.PrefetchScalarGridSpec(
            num_scalar_prefetch=1,
            grid=(last - first,),
            in_specs=[HERE] * n_in,
            out_specs=pl.BlockSpec((tile, width), lambda j, me: (j + first, 0)),
            scratch_shapes=[
                pltpu.VMEM((total, slot_width), jnp.bfloat16),
                pltpu.VMEM((total, part_width), jnp.bfloat16),
                pltpu.SemaphoreType.DMA((len(slots) + len(parts),)),
            ],
        ),
        out_shape=jax.ShapeDtypeStruct((tall, width), jnp.bfloat16),
        input_output_aliases={n_in: 0} if into else {},
        compiler_params=pltpu.CompilerParams(vmem_limit_bytes=40 * MIB),
        cost_estimate=NO_COST,
    )(me, *slots, *parts, *into)


class Program:
    def __init__(self, token):
        self.token = token

    def placed(self, values):
        return lax.optimization_barrier((*values, self.token))[:-1]

    def passed(self, values):
        *values, self.token = lax.optimization_barrier((*values, self.token))
        return values

    def start(self, value, axis, pairs):
        (value,) = self.placed([value])
        return lax.ppermute(value, axis, pairs)

    def wait(self, moving):
        return self.passed([moving])[0]

    def compute(self, step, *values):
        leaves, tree = jax.tree.flatten(step(*self.placed(values)))
        return jax.tree.unflatten(tree, self.passed(leaves))


def shards(sizes, tokens, w_in, w_out, spike_gain, cotangent):
    n_row, n_col, n_dp = sizes["row"], sizes["col"], sizes["dp"]
    chips = n_col // CORES
    chunks = CHUNKS if n_row % CHUNKS == 0 else 1
    per = n_row // chunks
    part = per * tokens.shape[0] // n_col
    me = lax.axis_index("col").astype(jnp.int32).reshape(1)
    run = Program(me)

    def row_start(value):
        return run.start(value, "row", [(i, (i + 1) % n_row) for i in range(n_row)])

    def core_start(value):
        return run.start(value, "col", [(i, i ^ 1) for i in range(n_col)])

    def chip_start(values):
        return [
            run.start(value, "col", [(i, i ^ (CORES * k)) for i in range(n_col)])
            for k, value in zip(range(1, chips), values)
        ]

    def half_start(value):
        return [
            run.start(value, "dp", [(d, (d + k) % n_dp) for d in range(n_dp)])
            for k in range(1, n_dp)
        ]

    def wait_all(moving):
        return [run.wait(value) for value in moving]

    def in_one_step(step):
        def taken(*values):
            def otherwise(*values):
                made = jax.eval_shape(step, *values)
                return jax.tree.map(lambda v: jnp.zeros(v.shape, v.dtype), made)

            return lax.cond(me[0] < n_col, step, otherwise, *values)

        taken.__name__ = step.__name__
        return taken

    def swap(value):
        return lax.ppermute(value, "col", [(i, i ^ 1) for i in range(n_col)])

    def part_sum(own, theirs, k):
        rows = slice(k * part, (k + 1) * part)
        return wide(own[rows]) + wide(theirs[rows])

    def forward(*slots):
        return project(me, chips, part, slots, w_in, False)

    def backward(*slots):
        return project(me, chips, part, slots, w_out, True)

    @in_one_step
    def chip_sums(own, for_sibling):
        theirs = swap(for_sibling)
        return [theirs] + [narrow(part_sum(own, theirs, k)) for k in range(1, chips)]

    def projected(step, slots):
        own, for_sibling = run.compute(step, *slots)
        return [own] + run.compute(chip_sums, own, for_sibling)

    @in_one_step
    def both_cores_now(*mine):
        return [swap(value) for value in mine]

    def expand_out(*parts):
        return expand(me, chips, part, parts, per, w_out, False)

    def expand_back(*parts):
        return expand(me, chips, part, parts, per, w_in, True)

    def spread_out(step, mine):
        parts = [*mine] + run.compute(both_cores_now, *mine)
        return run.compute(step, *parts), parts

    def whole(own, theirs, arrived):
        total = part_sum(own, theirs, 0)
        for value in arrived:
            total = total + wide(value)
        return total

    def fire(own, theirs, *arrived):
        total, slope = spike_parts(whole(own, theirs, arrived), spike_gain)
        return narrow(total), slope

    def slope_back(slope, own, theirs, *arrived):
        return narrow(whole(own, theirs, arrived) * slope)

    def ring_add(arrived, slot):
        return narrow(wide(arrived) + wide(slot))

    def weight_step(parts_left, share, shares):
        n_into = 1 if share > 0 else 0

        def weights(*values):
            into, values = values[:n_into], values[n_into:]
            slots, parts = values[:n_all], values[n_all:]
            span = (share, shares)
            return weight_product(me, part, chips, slots, parts, parts_left, span, into)

        return weights

    n_all = n_row * n_dp
    tok, cot, outs, back, summed = [], [], [], [], []

    def row_lane():
        for own, slots in ((tokens, tok), (cotangent, cot)):
            slots.append(own)
            for _ in range(n_row - 1):
                moving = row_start(slots[-1])
                yield
                slots.append(run.wait(moving))
        for slots in (outs, back):
            held = slots[1 % n_row]
            for s in range(2, n_row + 1):
                moving = row_start(held)
                yield
                held = run.compute(ring_add, run.wait(moving), slots[s % n_row])
            summed.append(held)

    row = row_lane()

    def turn():
        next(row, None)

    def until(slots, count):
        while len(slots) < count:
            turn()

    first, second = list(range(per)), list(range(per, n_row))
    far = {}
    spikes, slopes, grads = [], [], []
    sources = {"tok": tok, "cot": cot, "spike": spikes, "grad": grads}

    def half_lane():
        queue = [("tok", s) for s in first] + [("spike", 0)]
        queue += [("tok", s) for s in second[:-1]]
        queue += [("spike", c) for c in range(1, chunks)]
        queue += [("cot", s) for s in first] + [("grad", 0)]
        queue += [("cot", s) for s in second[:-1]]
        queue += [("grad", c) for c in range(1, chunks)]
        queue += [("cot", second[-1]), ("tok", second[-1])]
        for kind, at in queue:
            moving = half_start(sources[kind][at])
            yield
            far[kind, at] = wait_all(moving)

    half = half_lane()

    def half_turn():
        next(half, None)

    def spreading(value):
        return value, chip_start([value] * (chips - 1))

    def both_cores(mine):
        return [core_start(value) for value in mine]

    def chunk(slots, c):
        return slots[c * per : (c + 1) * per]

    turn()
    half_turn()
    until(tok, per)
    own, theirs, *sums = projected(forward, chunk(tok, 0))
    moving = chip_start(sums)
    half_turn()
    until(tok, n_row - 1)
    spike, slope = run.compute(fire, own, theirs, *wait_all(moving))
    spikes.append(spike)
    slopes.append(slope)
    gather = spreading(spike)
    half_turn()
    until(tok, n_row)

    grad_partials, grad_sums, mine, spike_all = [], [], [], []

    def project_back(c):
        until(cot, (c + 1) * per)
        own, theirs, *sums = projected(backward, chunk(cot, c))
        grad_partials.append((own, theirs))
        grad_sums.append(sums)

    def expanded(c):
        slots, parts = spread_out(expand_out, mine[c])
        outs.extend(slots)
        spike_all.extend(parts)

    for c in range(1, chunks):
        own, theirs, *sums = projected(forward, chunk(tok, c))
        mine.append([gather[0]] + wait_all(gather[1]))
        moving = chip_start(sums)
        half_turn()
        if c + 1 == chunks:
            project_back(0)
        spike, slope = run.compute(fire, own, theirs, *wait_all(moving))
        spikes.append(spike)
        slopes.append(slope)
        gather = spreading(spike)
        half_turn()
        expanded(c - 1)
        half_turn()
    if chunks == 1:
        project_back(0)
    until(cot, n_row - 1)
    mine.append([gather[0]] + wait_all(gather[1]))
    grad_moving = chip_start(grad_sums[0])
    expanded(chunks - 1)
    half_turn()
    until(cot, n_row)

    grad_all = []
    for c in range(chunks):
        grad = run.compute(
            slope_back, slopes[c], *grad_partials[c], *wait_all(grad_moving)
        )
        grads.append(grad)
        gather = spreading(grad)
        if c + 1 < chunks:
            project_back(c + 1)
        else:
            turn()
            half_turn()
        grad_mine = [gather[0]] + wait_all(gather[1])
        if c + 1 < chunks:
            grad_moving = chip_start(grad_sums[c + 1])
            turn()
        else:
            far_moving = chip_start(far["spike", 0][:1] * (chips - 1))
        if c + 1 < chunks:
            half_turn()
        slots, parts = spread_out(expand_back, grad_mine)
        back.extend(slots)
        grad_all.extend(parts)
        half_turn()

    todo = [
        (kind, c, h)
        for kind in ("spike", "grad")
        for h in range(n_dp - 1)
        for c in range(chunks)
    ]
    spread = {"spike": [], "grad": []}
    waiting = None

    def settle():
        if waiting is not None:
            kind, held, others = waiting
            spread[kind].extend(held + wait_all(others))

    def every(kind, slots):
        return slots + [far[kind, s][h] for h in range(n_dp - 1) for s in range(n_row)]

    def gradient(parts_left, share, shares, *into):
        kind, slots, parts = (
            ("spike", every("cot", cot), spike_all)
            if parts_left
            else ("grad", every("tok", tok), grad_all)
        )
        step = weight_step(parts_left, share, shares)
        return run.compute(step, *into, *slots, *parts, *spread[kind])

    spikes_last = len(todo) // 2 - 1
    weight_out = None
    for i, (kind, c, h) in enumerate(todo):
        held = [far[kind, c][h]] + wait_all(far_moving)
        others = both_cores(held)
        if i + 1 < len(todo):
            kind_next, c_next, h_next = todo[i + 1]
            while (kind_next, c_next) not in far:
                half_turn()
            far_moving = chip_start([far[kind_next, c_next][h_next]] * (chips - 1))
        settle()
        waiting = (kind, held, others)
        if i < spikes_last:
            turn()
            half_turn()
        elif i == spikes_last:
            settle()
            waiting = None
            while ("cot", n_row - 1) not in far:
                half_turn()
            weight_out = gradient(True, 0, 2)
            half_turn()
        elif i == spikes_last + 1:
            turn()
            weight_out = gradient(True, 1, 2, weight_out)
        else:
            turn()
    settle()
    while ("tok", n_row - 1) not in far:
        half_turn()
    weight_in = gradient(False, 0, 1)
    while len(summed) < 2:
        turn()
    return (summed[0], summed[1], weight_in, weight_out)


def solution(mesh):
    placed = (
        P(("dp", "row"), "col"),
        P("col", "row"),
        P("row", "col"),
        P("row"),
        P(("dp", "row"), "col"),
    )

    def program(*args):
        return shards(mesh.shape, *args)

    return jax.shard_map(
        program,
        mesh=mesh,
        in_specs=placed,
        out_specs=(
            P(("dp", "row"), "col"),
            P(("dp", "row"), "col"),
            P("col", "row"),
            P("row", "col"),
        ),
        check_vma=False,
    )
```

```python
import functools

import jax
import jax.numpy as jnp
from jax import lax
from jax.experimental import pallas as pl
from jax.experimental.pallas import tpu as pltpu
from jax.sharding import PartitionSpec as P

LEVELS = 4
CORES = 2
CHUNKS = 2
MIB = 1 << 20
AHEAD = 3
SPLIT = 4


sharpness = 4.0


def spike_parts(potential, gain):
    scaled = potential * gain[None, :]
    total = jnp.zeros_like(scaled)
    slope = jnp.zeros_like(scaled)
    for level in range(LEVELS):
        sig = jax.nn.sigmoid(sharpness * (scaled - (level + 0.5)))
        total = total + sig
        slope = slope + sig * (1.0 - sig)
    return (total, slope * (sharpness * gain[None, :]))


def wide(value):
    return value.astype(jnp.float32)


def narrow(value):
    return value.astype(jnp.bfloat16)


def tile_of(size, most):
    best = 128
    for tile in range(128, most + 1, 128):
        if size % tile == 0:
            best = tile
    return best


def product(left, right, contract):
    return lax.dot_general(
        left, right, (contract, ((), ())), preferred_element_type=jnp.float32
    )


HERE = pl.BlockSpec(memory_space=pl.ANY)
NO_COST = pl.CostEstimate(flops=0, bytes_accessed=0, transcendentals=0)
FAST = pl.BlockSpec(memory_space=pltpu.VMEM)


def copies_of(pairs, sems):
    return [
        pltpu.make_async_copy(source, target, sems.at[i])
        for i, (source, target) in enumerate(pairs)
    ]


def start_all(copies):
    for copy in copies:
        copy.start()


def finish_all(copies):
    for copy in copies:
        copy.wait()


def slot_places(slots, held):
    rows = slots[0].shape[0]
    return [(slot, held.at[pl.ds(i * rows, rows)]) for i, slot in enumerate(slots)]


def plain_rows(me, away_core, away_chip, rows, first):
    core = jnp.bitwise_xor(lax.rem(me, CORES), away_core)
    chip = jnp.bitwise_xor(lax.div(me, CORES), away_chip)
    return first + (chip * CORES + core) * rows


def gathered_places(me, chips, rows, parts, held):
    places = []
    for i, value in enumerate(parts):
        chunk, at = divmod(i, CORES * chips)
        first = chunk * CORES * chips * rows
        start = plain_rows(me, at // chips, at % chips, rows, first)
        places.append((value, held.at[pl.ds(pl.multiple_of(start, rows), rows)]))
    return places


def tile_copies(weight, tiles, sems, j, transposed):
    at, copies = j % AHEAD, []
    depth, width = tiles.shape[1:]
    rows = depth // SPLIT
    for i in range(SPLIT):
        part = pl.ds(i * rows, rows)
        if transposed:
            source = weight.at[pl.ds(j * depth + i * rows, rows)]
        else:
            source = weight.at[part, pl.ds(j * width, width)]
        copies.append(
            pltpu.make_async_copy(source, tiles.at[at, part], sems.at[at, i])
        )
    return copies


def tile_scratch(weight, tile, transposed):
    shape = (tile, weight.shape[1]) if transposed else (weight.shape[0], tile)
    return [
        pltpu.VMEM((AHEAD, *shape), jnp.bfloat16),
        pltpu.SemaphoreType.DMA((AHEAD, SPLIT)),
    ]


def product_kernel(place, transposed, n_in, n_out, me, *refs):
    sources, weight = refs[:n_in], refs[n_in]
    outs = refs[n_in + 1 : n_in + 1 + n_out]
    held, sems, tiles, tile_sems = refs[n_in + 1 + n_out :]
    contract = ((1,), (1,)) if transposed else ((1,), (0,))
    tile = tiles.shape[1 if transposed else 2]
    count = weight.shape[0 if transposed else 1] // tile
    copies = copies_of(place(me[0], sources, held), sems)
    start_all(copies)
    moving = [tile_copies(weight, tiles, tile_sems, j, transposed) for j in range(count)]
    for j in range(min(AHEAD - 1, count)):
        start_all(moving[j])
    finish_all(copies)
    for j in range(count):
        if j + AHEAD - 1 < count:
            start_all(moving[j + AHEAD - 1])
        finish_all(moving[j])
        where = slice(j * tile, (j + 1) * tile)
        result = narrow(product(held[...], tiles[j % AHEAD], contract))
        first = 0
        for out in outs:
            rows = out.shape[0]
            out[:, where] = result[first : first + rows]
            first += rows


def product_call(me, place, sources, n_copies, weight, transposed, out_rows):
    depth = sources[0].shape[1]
    width = weight.shape[0 if transposed else 1]
    return pl.pallas_call(
        functools.partial(
            product_kernel, place, transposed, len(sources), len(out_rows)
        ),
        in_specs=[pl.BlockSpec(memory_space=pltpu.SMEM)]
        + [HERE] * (len(sources) + 1),
        out_specs=[FAST] * len(out_rows),
        scratch_shapes=[
            pltpu.VMEM((sum(out_rows), depth), jnp.bfloat16),
            pltpu.SemaphoreType.DMA((n_copies,)),
            *tile_scratch(weight, tile_of(width, 512), transposed),
        ],
        out_shape=[jax.ShapeDtypeStruct((rows, width), jnp.bfloat16) for rows in out_rows],
        compiler_params=pltpu.CompilerParams(vmem_limit_bytes=18 * MIB),
        cost_estimate=NO_COST,
    )(me, *sources, pltpu.with_memory_space_constraint(weight, pltpu.HBM))


def project(me, chips, rows, slots, weight, transposed):
    total = sum(s.shape[0] for s in slots)
    height = slots[0].shape[0]
    piece = min(rows, height)

    def place(me, slots, held):
        places = []
        for first in range(0, total, piece):
            part, within = divmod(first, rows)
            core = jnp.bitwise_xor(lax.rem(me, CORES), part % CORES)
            chip = jnp.bitwise_xor(lax.div(me, CORES), part // CORES)
            at = pl.multiple_of((core * chips + chip) * rows + within, piece)
            source = slots[first // height].at[pl.ds(first % height, piece)]
            places.append((source, held.at[pl.ds(at, piece)]))
        return places

    cut = total // CORES
    out_rows = [cut] * CORES
    copies = total // piece
    return product_call(me, place, slots, copies, weight, transposed, out_rows)


def expand(me, chips, rows, parts, n_slots, weight, transposed):
    def place(me, parts, held):
        return gathered_places(me, chips, rows, parts, held)

    out_rows = [CORES * chips * rows // n_slots] * n_slots
    return product_call(me, place, parts, len(parts), weight, transposed, out_rows)


def weight_kernel(rows, chips, parts_left, n_slots, n_parts, tile, first, me, *refs):
    slots, parts = refs[:n_slots], refs[n_slots : n_slots + n_parts]
    out, held_slots, held_parts, sems = refs[-4:]
    step = pl.program_id(0) + first

    @pl.when(pl.program_id(0) == 0)
    def _():
        places = slot_places(slots, held_slots)
        places += gathered_places(me[0], chips, rows, parts, held_parts)
        copies = copies_of(places, sems)
        start_all(copies)
        finish_all(copies)

    left, right = (held_parts, held_slots) if parts_left else (held_slots, held_parts)
    columns = left[:, pl.ds(pl.multiple_of(step * tile, tile), tile)]
    out[...] = narrow(product(columns, right[...], ((0,), (0,))))


def weight_product(me, rows, chips, slots, parts, parts_left, span=(0, 1), into=()):
    total = sum(s.shape[0] for s in slots)
    slot_width, part_width = slots[0].shape[1], parts[0].shape[1]
    tall, width = (part_width, slot_width) if parts_left else (slot_width, part_width)
    tile = tile_of(tall, 512)
    share, shares = span
    first, last = (tall // tile * at // shares for at in (share, share + 1))
    n_in = len(slots) + len(parts) + len(into)
    return pl.pallas_call(
        functools.partial(
            weight_kernel, rows, chips, parts_left, len(slots), len(parts), tile, first
        ),
        grid_spec=pltpu.PrefetchScalarGridSpec(
            num_scalar_prefetch=1,
            grid=(last - first,),
            in_specs=[HERE] * n_in,
            out_specs=pl.BlockSpec((tile, width), lambda j, me: (j + first, 0)),
            scratch_shapes=[
                pltpu.VMEM((total, slot_width), jnp.bfloat16),
                pltpu.VMEM((total, part_width), jnp.bfloat16),
                pltpu.SemaphoreType.DMA((len(slots) + len(parts),)),
            ],
        ),
        out_shape=jax.ShapeDtypeStruct((tall, width), jnp.bfloat16),
        input_output_aliases={n_in: 0} if into else {},
        compiler_params=pltpu.CompilerParams(vmem_limit_bytes=40 * MIB),
        cost_estimate=NO_COST,
    )(me, *slots, *parts, *into)


class Program:
    def __init__(self, token):
        self.token = token

    def placed(self, values):
        return lax.optimization_barrier((*values, self.token))[:-1]

    def passed(self, values):
        *values, self.token = lax.optimization_barrier((*values, self.token))
        return values

    def start(self, value, axis, pairs):
        (value,) = self.placed([value])
        return lax.ppermute(value, axis, pairs)

    def wait(self, moving):
        return self.passed([moving])[0]

    def compute(self, step, *values):
        leaves, tree = jax.tree.flatten(step(*self.placed(values)))
        return jax.tree.unflatten(tree, self.passed(leaves))


def shards(sizes, tokens, w_in, w_out, spike_gain, cotangent):
    n_row, n_col, n_dp = sizes["row"], sizes["col"], sizes["dp"]
    chips = n_col // CORES
    chunks = CHUNKS if n_row % CHUNKS == 0 else 1
    per = n_row // chunks
    part = per * tokens.shape[0] // n_col
    me = lax.axis_index("col").astype(jnp.int32).reshape(1)
    run = Program(me)

    def row_start(value):
        return run.start(value, "row", [(i, (i + 1) % n_row) for i in range(n_row)])

    def core_start(value):
        return run.start(value, "col", [(i, i ^ 1) for i in range(n_col)])

    def chip_start(values):
        return [
            run.start(value, "col", [(i, i ^ (CORES * k)) for i in range(n_col)])
            for k, value in zip(range(1, chips), values)
        ]

    def half_start(value):
        return [
            run.start(value, "dp", [(d, (d + k) % n_dp) for d in range(n_dp)])
            for k in range(1, n_dp)
        ]

    def wait_all(moving):
        return [run.wait(value) for value in moving]

    def in_one_step(step):
        def taken(*values):
            def otherwise(*values):
                made = jax.eval_shape(step, *values)
                return jax.tree.map(lambda v: jnp.zeros(v.shape, v.dtype), made)

            return lax.cond(me[0] < n_col, step, otherwise, *values)

        taken.__name__ = step.__name__
        return taken

    def swap(value):
        return lax.ppermute(value, "col", [(i, i ^ 1) for i in range(n_col)])

    def part_sum(own, theirs, k):
        rows = slice(k * part, (k + 1) * part)
        return wide(own[rows]) + wide(theirs[rows])

    def forward(*slots):
        return project(me, chips, part, slots, w_in, False)

    def backward(*slots):
        return project(me, chips, part, slots, w_out, True)

    @in_one_step
    def chip_sums(own, for_sibling):
        theirs = swap(for_sibling)
        return [theirs] + [narrow(part_sum(own, theirs, k)) for k in range(1, chips)]

    def projected(step, slots):
        own, for_sibling = run.compute(step, *slots)
        return [own] + run.compute(chip_sums, own, for_sibling)

    @in_one_step
    def both_cores_now(*mine):
        return [swap(value) for value in mine]

    def expand_out(*parts):
        return expand(me, chips, part, parts, per, w_out, False)

    def expand_back(*parts):
        return expand(me, chips, part, parts, per, w_in, True)

    def spread_out(step, mine):
        parts = [*mine] + run.compute(both_cores_now, *mine)
        return run.compute(step, *parts), parts

    def whole(own, theirs, arrived):
        total = part_sum(own, theirs, 0)
        for value in arrived:
            total = total + wide(value)
        return total

    def fire(own, theirs, *arrived):
        total, slope = spike_parts(whole(own, theirs, arrived), spike_gain)
        return narrow(total), slope

    def slope_back(slope, own, theirs, *arrived):
        return narrow(whole(own, theirs, arrived) * slope)

    def ring_add(arrived, slot):
        return narrow(wide(arrived) + wide(slot))

    def weight_step(parts_left, share, shares):
        n_into = 1 if share > 0 else 0

        def weights(*values):
            into, values = values[:n_into], values[n_into:]
            slots, parts = values[:n_all], values[n_all:]
            span = (share, shares)
            return weight_product(me, part, chips, slots, parts, parts_left, span, into)

        return weights

    n_all = n_row * n_dp
    tok, cot, outs, back, summed = [], [], [], [], []

    def row_lane():
        for own, slots in ((tokens, tok), (cotangent, cot)):
            slots.append(own)
            for _ in range(n_row - 1):
                moving = row_start(slots[-1])
                yield
                slots.append(run.wait(moving))
                if slots is cot:
                    sources["cot"].append(slots[-1])
        for slots in (outs, back):
            held = slots[1 % n_row]
            for s in range(2, n_row + 1):
                moving = row_start(held)
                yield
                held = run.compute(ring_add, run.wait(moving), slots[s % n_row])
            summed.append(held)

    row = row_lane()

    def turn():
        next(row, None)

    def until(slots, count):
        while len(slots) < count:
            turn()

    first, second = list(range(per)), list(range(per, n_row))
    far = {}
    spikes, slopes, grads = [], [], []
    sources = {"tok": tok, "cot": [cotangent], "spike": spikes, "grad": grads}

    def half_lane():
        queue = [[("tok", 0), ("cot", 0)]] + [[("tok", s)] for s in first[1:]]
        queue += [[("spike", 0)]] + [[("tok", s)] for s in second[:-1]]
        queue += [[("spike", c)] for c in range(1, chunks)]
        queue += [[("cot", s)] for s in first[1:]] + [[("grad", 0)]]
        queue += [[("cot", s)] for s in second]
        queue += [[("grad", c)] for c in range(1, chunks)]
        queue += [[("tok", s)] for s in second[-1:]]
        for group in queue:
            moving = [half_start(sources[kind][at]) for kind, at in group]
            yield
            for place, values in zip(group, moving):
                far[place] = wait_all(values)

    half = half_lane()

    def half_turn():
        next(half, None)

    def spreading(value):
        return value, chip_start([value] * (chips - 1))

    def both_cores(mine):
        return [core_start(value) for value in mine]

    def chunk(slots, c):
        return slots[c * per : (c + 1) * per]

    turn()
    half_turn()
    until(tok, per)
    own, theirs, *sums = projected(forward, chunk(tok, 0))
    moving = chip_start(sums)
    half_turn()
    until(tok, n_row - 1)
    spike, slope = run.compute(fire, own, theirs, *wait_all(moving))
    spikes.append(spike)
    slopes.append(slope)
    gather = spreading(spike)
    half_turn()
    until(tok, n_row)

    grad_partials, grad_sums, mine, spike_all = [], [], [], []

    def project_back(c):
        until(cot, (c + 1) * per)
        own, theirs, *sums = projected(backward, chunk(cot, c))
        grad_partials.append((own, theirs))
        grad_sums.append(sums)

    def expanded(c):
        slots, parts = spread_out(expand_out, mine[c])
        outs.extend(slots)
        spike_all.extend(parts)

    for c in range(1, chunks):
        own, theirs, *sums = projected(forward, chunk(tok, c))
        mine.append([gather[0]] + wait_all(gather[1]))
        moving = chip_start(sums)
        half_turn()
        if c + 1 == chunks:
            project_back(0)
        spike, slope = run.compute(fire, own, theirs, *wait_all(moving))
        spikes.append(spike)
        slopes.append(slope)
        gather = spreading(spike)
        half_turn()
        expanded(c - 1)
        half_turn()
    if chunks == 1:
        project_back(0)
    until(cot, n_row - 1)
    mine.append([gather[0]] + wait_all(gather[1]))
    grad_moving = chip_start(grad_sums[0])
    expanded(chunks - 1)
    until(cot, n_row)

    grad_all = []
    for c in range(chunks):
        grad = run.compute(
            slope_back, slopes[c], *grad_partials[c], *wait_all(grad_moving)
        )
        grads.append(grad)
        gather = spreading(grad)
        if c + 1 < chunks:
            half_turn()
            project_back(c + 1)
        else:
            turn()
        grad_mine = [gather[0]] + wait_all(gather[1])
        if c + 1 < chunks:
            grad_moving = chip_start(grad_sums[c + 1])
            turn()
        else:
            far_moving = chip_start(far["spike", 0][:1] * (chips - 1))
        if c + 1 < chunks:
            half_turn()
        slots, parts = spread_out(expand_back, grad_mine)
        back.extend(slots)
        grad_all.extend(parts)
        half_turn()

    todo = [
        (kind, c, h)
        for kind in ("spike", "grad")
        for h in range(n_dp - 1)
        for c in range(chunks)
    ]
    spread = {"spike": [], "grad": []}
    waiting = None

    def settle():
        if waiting is not None:
            kind, held, others = waiting
            spread[kind].extend(held + wait_all(others))

    def every(kind, slots):
        return slots + [far[kind, s][h] for h in range(n_dp - 1) for s in range(n_row)]

    def gradient(parts_left, share, shares, *into):
        kind, slots, parts = (
            ("spike", every("cot", cot), spike_all)
            if parts_left
            else ("grad", every("tok", tok), grad_all)
        )
        step = weight_step(parts_left, share, shares)
        return run.compute(step, *into, *slots, *parts, *spread[kind])

    spikes_last = len(todo) // 2 - 1
    weight_out = None
    for i, (kind, c, h) in enumerate(todo):
        held = [far[kind, c][h]] + wait_all(far_moving)
        others = both_cores(held)
        if i + 1 < len(todo):
            kind_next, c_next, h_next = todo[i + 1]
            while (kind_next, c_next) not in far:
                half_turn()
            far_moving = chip_start([far[kind_next, c_next][h_next]] * (chips - 1))
        settle()
        waiting = (kind, held, others)
        if i < spikes_last:
            turn()
            half_turn()
        elif i == spikes_last:
            settle()
            waiting = None
            while ("cot", n_row - 1) not in far:
                half_turn()
            weight_out = gradient(True, 0, 2)
            half_turn()
        elif i == spikes_last + 1:
            turn()
            weight_out = gradient(True, 1, 2, weight_out)
        else:
            turn()
    settle()
    while ("tok", n_row - 1) not in far:
        half_turn()
    weight_in = gradient(False, 0, 1)
    while len(summed) < 2:
        turn()
    return (summed[0], summed[1], weight_in, weight_out)


def solution(mesh):
    placed = (
        P(("dp", "row"), "col"),
        P("col", "row"),
        P("row", "col"),
        P("row"),
        P(("dp", "row"), "col"),
    )

    def program(*args):
        return shards(mesh.shape, *args)

    return jax.shard_map(
        program,
        mesh=mesh,
        in_specs=placed,
        out_specs=(
            P(("dp", "row"), "col"),
            P(("dp", "row"), "col"),
            P("col", "row"),
            P("row", "col"),
        ),
        check_vma=False,
    )
```

```python
import functools

import jax
import jax.numpy as jnp
from jax import lax
from jax.experimental import pallas as pl
from jax.experimental.pallas import tpu as pltpu
from jax.sharding import PartitionSpec as P

LEVELS = 4
CORES = 2
CHUNKS = 2
MIB = 1 << 20
AHEAD = 3
SPLIT = 4


sharpness = 4.0


def spike_parts(potential, gain):
    scaled = potential * gain[None, :]
    total = jnp.zeros_like(scaled)
    slope = jnp.zeros_like(scaled)
    for level in range(LEVELS):
        sig = jax.nn.sigmoid(sharpness * (scaled - (level + 0.5)))
        total = total + sig
        slope = slope + sig * (1.0 - sig)
    return (total, slope * (sharpness * gain[None, :]))


def wide(value):
    return value.astype(jnp.float32)


def narrow(value):
    return value.astype(jnp.bfloat16)


def tile_of(size, most):
    best = 128
    for tile in range(128, most + 1, 128):
        if size % tile == 0:
            best = tile
    return best


def product(left, right, contract):
    return lax.dot_general(
        left, right, (contract, ((), ())), preferred_element_type=jnp.float32
    )


HERE = pl.BlockSpec(memory_space=pl.ANY)
NO_COST = pl.CostEstimate(flops=0, bytes_accessed=0, transcendentals=0)
FAST = pl.BlockSpec(memory_space=pltpu.VMEM)


def copies_of(pairs, sems):
    return [
        pltpu.make_async_copy(source, target, sems.at[i])
        for i, (source, target) in enumerate(pairs)
    ]


def start_all(copies):
    for copy in copies:
        copy.start()


def finish_all(copies):
    for copy in copies:
        copy.wait()


def slot_places(slots, held):
    rows = slots[0].shape[0]
    return [(slot, held.at[pl.ds(i * rows, rows)]) for i, slot in enumerate(slots)]


def plain_rows(me, away_core, away_chip, rows, first):
    core = jnp.bitwise_xor(lax.rem(me, CORES), away_core)
    chip = jnp.bitwise_xor(lax.div(me, CORES), away_chip)
    return first + (chip * CORES + core) * rows


def gathered_places(me, chips, rows, parts, held):
    places = []
    for i, value in enumerate(parts):
        chunk, at = divmod(i, CORES * chips)
        first = chunk * CORES * chips * rows
        start = plain_rows(me, at // chips, at % chips, rows, first)
        places.append((value, held.at[pl.ds(pl.multiple_of(start, rows), rows)]))
    return places


def tile_copies(weight, tiles, sems, j, transposed):
    at, copies = j % AHEAD, []
    depth, width = tiles.shape[1:]
    rows = depth // SPLIT
    for i in range(SPLIT):
        part = pl.ds(i * rows, rows)
        if transposed:
            source = weight.at[pl.ds(j * depth + i * rows, rows)]
        else:
            source = weight.at[part, pl.ds(j * width, width)]
        copies.append(
            pltpu.make_async_copy(source, tiles.at[at, part], sems.at[at, i])
        )
    return copies


def tile_scratch(weight, tile, transposed):
    shape = (tile, weight.shape[1]) if transposed else (weight.shape[0], tile)
    return [
        pltpu.VMEM((AHEAD, *shape), jnp.bfloat16),
        pltpu.SemaphoreType.DMA((AHEAD, SPLIT)),
    ]


def product_kernel(place, transposed, n_in, n_out, me, *refs):
    sources, weight = refs[:n_in], refs[n_in]
    outs = refs[n_in + 1 : n_in + 1 + n_out]
    held, sems, tiles, tile_sems = refs[n_in + 1 + n_out :]
    contract = ((1,), (1,)) if transposed else ((1,), (0,))
    tile = tiles.shape[1 if transposed else 2]
    count = weight.shape[0 if transposed else 1] // tile
    copies = copies_of(place(me[0], sources, held), sems)
    start_all(copies)
    moving = [tile_copies(weight, tiles, tile_sems, j, transposed) for j in range(count)]
    for j in range(min(AHEAD - 1, count)):
        start_all(moving[j])
    finish_all(copies)
    for j in range(count):
        if j + AHEAD - 1 < count:
            start_all(moving[j + AHEAD - 1])
        finish_all(moving[j])
        where = slice(j * tile, (j + 1) * tile)
        result = narrow(product(held[...], tiles[j % AHEAD], contract))
        first = 0
        for out in outs:
            rows = out.shape[0]
            out[:, where] = result[first : first + rows]
            first += rows


def product_call(me, place, sources, n_copies, weight, transposed, out_rows):
    depth = sources[0].shape[1]
    width = weight.shape[0 if transposed else 1]
    return pl.pallas_call(
        functools.partial(
            product_kernel, place, transposed, len(sources), len(out_rows)
        ),
        in_specs=[pl.BlockSpec(memory_space=pltpu.SMEM)]
        + [HERE] * (len(sources) + 1),
        out_specs=[FAST] * len(out_rows),
        scratch_shapes=[
            pltpu.VMEM((sum(out_rows), depth), jnp.bfloat16),
            pltpu.SemaphoreType.DMA((n_copies,)),
            *tile_scratch(weight, tile_of(width, 512), transposed),
        ],
        out_shape=[jax.ShapeDtypeStruct((rows, width), jnp.bfloat16) for rows in out_rows],
        compiler_params=pltpu.CompilerParams(vmem_limit_bytes=18 * MIB),
        cost_estimate=NO_COST,
    )(me, *sources, pltpu.with_memory_space_constraint(weight, pltpu.HBM))


def project(me, chips, rows, slots, weight, transposed):
    total = sum(s.shape[0] for s in slots)
    height = slots[0].shape[0]
    piece = min(rows, height)

    def place(me, slots, held):
        places = []
        for first in range(0, total, piece):
            part, within = divmod(first, rows)
            core = jnp.bitwise_xor(lax.rem(me, CORES), part % CORES)
            chip = jnp.bitwise_xor(lax.div(me, CORES), part // CORES)
            at = pl.multiple_of((core * chips + chip) * rows + within, piece)
            source = slots[first // height].at[pl.ds(first % height, piece)]
            places.append((source, held.at[pl.ds(at, piece)]))
        return places

    cut = total // CORES
    out_rows = [cut] * CORES
    copies = total // piece
    return product_call(me, place, slots, copies, weight, transposed, out_rows)


def expand(me, chips, rows, parts, n_slots, weight, transposed):
    def place(me, parts, held):
        return gathered_places(me, chips, rows, parts, held)

    out_rows = [CORES * chips * rows // n_slots] * n_slots
    return product_call(me, place, parts, len(parts), weight, transposed, out_rows)


def weight_kernel(rows, chips, parts_left, n_slots, n_parts, tile, first, me, *refs):
    slots, parts = refs[:n_slots], refs[n_slots : n_slots + n_parts]
    out, held_slots, held_parts, sems = refs[-4:]
    step = pl.program_id(0) + first

    @pl.when(pl.program_id(0) == 0)
    def _():
        places = slot_places(slots, held_slots)
        places += gathered_places(me[0], chips, rows, parts, held_parts)
        copies = copies_of(places, sems)
        start_all(copies)
        finish_all(copies)

    left, right = (held_parts, held_slots) if parts_left else (held_slots, held_parts)
    columns = left[:, pl.ds(pl.multiple_of(step * tile, tile), tile)]
    out[...] = narrow(product(columns, right[...], ((0,), (0,))))


def weight_product(me, rows, chips, slots, parts, parts_left, span=(0, 1), into=()):
    total = sum(s.shape[0] for s in slots)
    slot_width, part_width = slots[0].shape[1], parts[0].shape[1]
    tall, width = (part_width, slot_width) if parts_left else (slot_width, part_width)
    tile = tile_of(tall, 512)
    share, shares = span
    first, last = (tall // tile * at // shares for at in (share, share + 1))
    n_in = len(slots) + len(parts) + len(into)
    return pl.pallas_call(
        functools.partial(
            weight_kernel, rows, chips, parts_left, len(slots), len(parts), tile, first
        ),
        grid_spec=pltpu.PrefetchScalarGridSpec(
            num_scalar_prefetch=1,
            grid=(last - first,),
            in_specs=[HERE] * n_in,
            out_specs=pl.BlockSpec((tile, width), lambda j, me: (j + first, 0)),
            scratch_shapes=[
                pltpu.VMEM((total, slot_width), jnp.bfloat16),
                pltpu.VMEM((total, part_width), jnp.bfloat16),
                pltpu.SemaphoreType.DMA((len(slots) + len(parts),)),
            ],
        ),
        out_shape=jax.ShapeDtypeStruct((tall, width), jnp.bfloat16),
        input_output_aliases={n_in: 0} if into else {},
        compiler_params=pltpu.CompilerParams(vmem_limit_bytes=40 * MIB),
        cost_estimate=NO_COST,
    )(me, *slots, *parts, *into)


class Program:
    def __init__(self, token):
        self.token = token

    def placed(self, values):
        return lax.optimization_barrier((*values, self.token))[:-1]

    def passed(self, values):
        *values, self.token = lax.optimization_barrier((*values, self.token))
        return values

    def start(self, value, axis, pairs):
        (value,) = self.placed([value])
        return lax.ppermute(value, axis, pairs)

    def wait(self, moving):
        return self.passed([moving])[0]

    def compute(self, step, *values):
        leaves, tree = jax.tree.flatten(step(*self.placed(values)))
        return jax.tree.unflatten(tree, self.passed(leaves))


def shards(sizes, tokens, w_in, w_out, spike_gain, cotangent):
    n_row, n_col, n_dp = sizes["row"], sizes["col"], sizes["dp"]
    chips = n_col // CORES
    chunks = CHUNKS if n_row % CHUNKS == 0 else 1
    per = n_row // chunks
    part = per * tokens.shape[0] // n_col
    me = lax.axis_index("col").astype(jnp.int32).reshape(1)
    run = Program(me)

    def row_start(value, by=1):
        return run.start(value, "row", [(i, (i + by) % n_row) for i in range(n_row)])

    def core_start(value):
        return run.start(value, "col", [(i, i ^ 1) for i in range(n_col)])

    def chip_start(values):
        return [
            run.start(value, "col", [(i, i ^ (CORES * k)) for i in range(n_col)])
            for k, value in zip(range(1, chips), values)
        ]

    def half_start(value):
        return [
            run.start(value, "dp", [(d, (d + k) % n_dp) for d in range(n_dp)])
            for k in range(1, n_dp)
        ]

    def wait_all(moving):
        return [run.wait(value) for value in moving]

    def in_one_step(step):
        def taken(*values):
            def otherwise(*values):
                made = jax.eval_shape(step, *values)
                return jax.tree.map(lambda v: jnp.zeros(v.shape, v.dtype), made)

            return lax.cond(me[0] < n_col, step, otherwise, *values)

        taken.__name__ = step.__name__
        return taken

    def swap(value):
        return lax.ppermute(value, "col", [(i, i ^ 1) for i in range(n_col)])

    def part_sum(own, theirs, k):
        rows = slice(k * part, (k + 1) * part)
        return wide(own[rows]) + wide(theirs[rows])

    def forward(*slots):
        return project(me, chips, part, slots, w_in, False)

    def backward(*slots):
        return project(me, chips, part, slots, w_out, True)

    @in_one_step
    def chip_sums(own, for_sibling):
        theirs = swap(for_sibling)
        return [theirs] + [narrow(part_sum(own, theirs, k)) for k in range(1, chips)]

    def projected(step, slots):
        own, for_sibling = run.compute(step, *slots)
        return [own] + run.compute(chip_sums, own, for_sibling)

    @in_one_step
    def both_cores_now(*mine):
        return [swap(value) for value in mine]

    def expand_out(*parts):
        return expand(me, chips, part, parts, per, w_out, False)

    def expand_back(*parts):
        return expand(me, chips, part, parts, per, w_in, True)

    def spread_out(step, mine):
        parts = [*mine] + run.compute(both_cores_now, *mine)
        return run.compute(step, *parts), parts

    def whole(own, theirs, arrived):
        total = part_sum(own, theirs, 0)
        for value in arrived:
            total = total + wide(value)
        return total

    def fire(own, theirs, *arrived):
        total, slope = spike_parts(whole(own, theirs, arrived), spike_gain)
        return narrow(total), slope

    def slope_back(slope, own, theirs, *arrived):
        return narrow(whole(own, theirs, arrived) * slope)

    def ring_add(arrived, slot):
        return narrow(wide(arrived) + wide(slot))

    def weight_step(parts_left, share, shares):
        n_into = 1 if share > 0 else 0

        def weights(*values):
            into, values = values[:n_into], values[n_into:]
            slots, parts = values[:n_all], values[n_all:]
            span = (share, shares)
            return weight_product(me, part, chips, slots, parts, parts_left, span, into)

        return weights

    n_all = n_row * n_dp
    tok, cot, outs, back, summed = [], [], [], [], []

    def row_lane():
        for own, slots in ((tokens, tok), (cotangent, cot)):
            slots.append(own)
            ahead, behind = own, own
            low, high, late = 1, n_row, []
            while low < high:
                both = low > 1 and high - low > 1
                moving = [row_start(ahead)] + ([row_start(behind, -1)] if both else [])
                yield
                ahead, *rest = [run.wait(value) for value in moving]
                slots.append(ahead)
                low += 1
                if both:
                    (behind,) = rest
                    late.insert(0, behind)
                    high -= 1
            slots.extend(late)
        for slots in (outs, back):
            held = slots[1 % n_row]
            for s in range(2, n_row + 1):
                moving = row_start(held)
                yield
                held = run.compute(ring_add, run.wait(moving), slots[s % n_row])
            summed.append(held)

    row = row_lane()

    def turn():
        next(row, None)

    def until(slots, count):
        while len(slots) < count:
            turn()

    first, second = list(range(per)), list(range(per, n_row))
    far = {}
    spikes, slopes, grads = [], [], []
    sources = {"tok": tok, "cot": cot, "spike": spikes, "grad": grads}

    def half_lane():
        queue = [[("tok", 0), ("cot", 0)]] + [[("tok", s)] for s in first[1:]]
        queue += [[("spike", 0)]] + [[("tok", s)] for s in second[:-1]]
        queue += [[("spike", c)] for c in range(1, chunks)]
        queue += [[("cot", s)] for s in first[1:]] + [[("grad", 0)]]
        queue += [[("cot", s)] for s in second]
        queue += [[("grad", c)] for c in range(1, chunks)]
        queue += [[("tok", s)] for s in second[-1:]]
        for group in queue:
            moving = [
                half_start(cotangent if (kind, at) == ("cot", 0) else sources[kind][at])
                for kind, at in group
            ]
            yield
            for place, values in zip(group, moving):
                far[place] = wait_all(values)

    half = half_lane()

    def half_turn():
        next(half, None)

    def spreading(value):
        return value, chip_start([value] * (chips - 1))

    def both_cores(mine):
        return [core_start(value) for value in mine]

    def chunk(slots, c):
        return slots[c * per : (c + 1) * per]

    turn()
    half_turn()
    until(tok, per)
    own, theirs, *sums = projected(forward, chunk(tok, 0))
    moving = chip_start(sums)
    half_turn()
    until(tok, n_row - 1)
    spike, slope = run.compute(fire, own, theirs, *wait_all(moving))
    spikes.append(spike)
    slopes.append(slope)
    gather = spreading(spike)
    half_turn()
    until(tok, n_row)

    grad_partials, grad_sums, mine, spike_all = [], [], [], []

    def project_back(c):
        until(cot, (c + 1) * per)
        own, theirs, *sums = projected(backward, chunk(cot, c))
        grad_partials.append((own, theirs))
        grad_sums.append(sums)

    def expanded(c):
        slots, parts = spread_out(expand_out, mine[c])
        outs.extend(slots)
        spike_all.extend(parts)

    for c in range(1, chunks):
        own, theirs, *sums = projected(forward, chunk(tok, c))
        mine.append([gather[0]] + wait_all(gather[1]))
        moving = chip_start(sums)
        half_turn()
        if c + 1 == chunks:
            project_back(0)
        spike, slope = run.compute(fire, own, theirs, *wait_all(moving))
        spikes.append(spike)
        slopes.append(slope)
        gather = spreading(spike)
        half_turn()
        expanded(c - 1)
        half_turn()
    if chunks == 1:
        project_back(0)
    until(cot, n_row - 1)
    mine.append([gather[0]] + wait_all(gather[1]))
    grad_moving = chip_start(grad_sums[0])
    expanded(chunks - 1)
    until(cot, n_row)

    grad_all = []
    for c in range(chunks):
        grad = run.compute(
            slope_back, slopes[c], *grad_partials[c], *wait_all(grad_moving)
        )
        grads.append(grad)
        gather = spreading(grad)
        if c + 1 < chunks:
            half_turn()
            project_back(c + 1)
        else:
            turn()
        grad_mine = [gather[0]] + wait_all(gather[1])
        if c + 1 < chunks:
            grad_moving = chip_start(grad_sums[c + 1])
            turn()
        else:
            far_moving = chip_start(far["spike", 0][:1] * (chips - 1))
        if c + 1 < chunks:
            half_turn()
        slots, parts = spread_out(expand_back, grad_mine)
        back.extend(slots)
        grad_all.extend(parts)
        half_turn()

    todo = [
        (kind, c, h)
        for kind in ("spike", "grad")
        for h in range(n_dp - 1)
        for c in range(chunks)
    ]
    spread = {"spike": [], "grad": []}
    waiting = None

    def settle():
        if waiting is not None:
            kind, held, others = waiting
            spread[kind].extend(held + wait_all(others))

    def every(kind, slots):
        return slots + [far[kind, s][h] for h in range(n_dp - 1) for s in range(n_row)]

    def gradient(parts_left, share, shares, *into):
        kind, slots, parts = (
            ("spike", every("cot", cot), spike_all)
            if parts_left
            else ("grad", every("tok", tok), grad_all)
        )
        step = weight_step(parts_left, share, shares)
        return run.compute(step, *into, *slots, *parts, *spread[kind])

    spikes_last = len(todo) // 2 - 1
    weight_out = None
    for i, (kind, c, h) in enumerate(todo):
        held = [far[kind, c][h]] + wait_all(far_moving)
        others = both_cores(held)
        if i + 1 < len(todo):
            kind_next, c_next, h_next = todo[i + 1]
            while (kind_next, c_next) not in far:
                half_turn()
            far_moving = chip_start([far[kind_next, c_next][h_next]] * (chips - 1))
        settle()
        waiting = (kind, held, others)
        if i < spikes_last:
            turn()
            half_turn()
        elif i == spikes_last:
            settle()
            waiting = None
            while ("cot", n_row - 1) not in far:
                half_turn()
            weight_out = gradient(True, 0, 2)
            half_turn()
        elif i == spikes_last + 1:
            turn()
            weight_out = gradient(True, 1, 2, weight_out)
        else:
            turn()
    settle()
    while ("tok", n_row - 1) not in far:
        half_turn()
    weight_in = gradient(False, 0, 1)
    while len(summed) < 2:
        turn()
    return (summed[0], summed[1], weight_in, weight_out)


def solution(mesh):
    placed = (
        P(("dp", "row"), "col"),
        P("col", "row"),
        P("row", "col"),
        P("row"),
        P(("dp", "row"), "col"),
    )

    def program(*args):
        return shards(mesh.shape, *args)

    return jax.shard_map(
        program,
        mesh=mesh,
        in_specs=placed,
        out_specs=(
            P(("dp", "row"), "col"),
            P(("dp", "row"), "col"),
            P("col", "row"),
            P("row", "col"),
        ),
        check_vma=False,
    )
```

```python
import functools

import jax
import jax.numpy as jnp
from jax import lax
from jax.experimental import pallas as pl
from jax.experimental.pallas import tpu as pltpu
from jax.sharding import PartitionSpec as P

LEVELS = 4
CORES = 2
CHUNKS = 2
MIB = 1 << 20
AHEAD = 3
SPLIT = 4


sharpness = 4.0


def spike_parts(potential, gain):
    scaled = potential * gain[None, :]
    total = jnp.zeros_like(scaled)
    slope = jnp.zeros_like(scaled)
    for level in range(LEVELS):
        sig = 0.5 + 0.5 * jnp.tanh(0.5 * sharpness * (scaled - (level + 0.5)))
        total = total + sig
        slope = slope + sig * (1.0 - sig)
    return (total, slope * (sharpness * gain[None, :]))


def wide(value):
    return value.astype(jnp.float32)


def narrow(value):
    return value.astype(jnp.bfloat16)


def tile_of(size, most):
    best = 128
    for tile in range(128, most + 1, 128):
        if size % tile == 0:
            best = tile
    return best


def product(left, right, contract):
    return lax.dot_general(
        left, right, (contract, ((), ())), preferred_element_type=jnp.float32
    )


HERE = pl.BlockSpec(memory_space=pl.ANY)
NO_COST = pl.CostEstimate(flops=0, bytes_accessed=0, transcendentals=0)
FAST = pl.BlockSpec(memory_space=pltpu.VMEM)


def copies_of(pairs, sems):
    return [
        pltpu.make_async_copy(source, target, sems.at[i])
        for i, (source, target) in enumerate(pairs)
    ]


def start_all(copies):
    for copy in copies:
        copy.start()


def finish_all(copies):
    for copy in copies:
        copy.wait()


def slot_places(slots, held):
    rows = slots[0].shape[0]
    return [(slot, held.at[pl.ds(i * rows, rows)]) for i, slot in enumerate(slots)]


def plain_rows(me, away_core, away_chip, rows, first):
    core = jnp.bitwise_xor(lax.rem(me, CORES), away_core)
    chip = jnp.bitwise_xor(lax.div(me, CORES), away_chip)
    return first + (chip * CORES + core) * rows


def gathered_places(me, chips, rows, parts, held):
    places = []
    for i, value in enumerate(parts):
        chunk, at = divmod(i, CORES * chips)
        first = chunk * CORES * chips * rows
        start = plain_rows(me, at // chips, at % chips, rows, first)
        places.append((value, held.at[pl.ds(pl.multiple_of(start, rows), rows)]))
    return places


def tile_copies(weight, tiles, sems, j, transposed):
    at, copies = j % AHEAD, []
    depth, width = tiles.shape[1:]
    rows = depth // SPLIT
    for i in range(SPLIT):
        part = pl.ds(i * rows, rows)
        if transposed:
            source = weight.at[pl.ds(j * depth + i * rows, rows)]
        else:
            source = weight.at[part, pl.ds(j * width, width)]
        copies.append(
            pltpu.make_async_copy(source, tiles.at[at, part], sems.at[at, i])
        )
    return copies


def tile_scratch(weight, tile, transposed):
    shape = (tile, weight.shape[1]) if transposed else (weight.shape[0], tile)
    return [
        pltpu.VMEM((AHEAD, *shape), jnp.bfloat16),
        pltpu.SemaphoreType.DMA((AHEAD, SPLIT)),
    ]


def product_kernel(place, transposed, n_in, n_out, me, *refs):
    sources, weight = refs[:n_in], refs[n_in]
    outs = refs[n_in + 1 : n_in + 1 + n_out]
    held, sems, tiles, tile_sems = refs[n_in + 1 + n_out :]
    contract = ((1,), (1,)) if transposed else ((1,), (0,))
    tile = tiles.shape[1 if transposed else 2]
    count = weight.shape[0 if transposed else 1] // tile
    copies = copies_of(place(me[0], sources, held), sems)
    start_all(copies)
    moving = [tile_copies(weight, tiles, tile_sems, j, transposed) for j in range(count)]
    for j in range(min(AHEAD - 1, count)):
        start_all(moving[j])
    finish_all(copies)
    for j in range(count):
        if j + AHEAD - 1 < count:
            start_all(moving[j + AHEAD - 1])
        finish_all(moving[j])
        where = slice(j * tile, (j + 1) * tile)
        result = narrow(product(held[...], tiles[j % AHEAD], contract))
        first = 0
        for out in outs:
            rows = out.shape[0]
            out[:, where] = result[first : first + rows]
            first += rows


def product_call(me, place, sources, n_copies, weight, transposed, out_rows):
    depth = sources[0].shape[1]
    width = weight.shape[0 if transposed else 1]
    return pl.pallas_call(
        functools.partial(
            product_kernel, place, transposed, len(sources), len(out_rows)
        ),
        in_specs=[pl.BlockSpec(memory_space=pltpu.SMEM)]
        + [HERE] * (len(sources) + 1),
        out_specs=[FAST] * len(out_rows),
        scratch_shapes=[
            pltpu.VMEM((sum(out_rows), depth), jnp.bfloat16),
            pltpu.SemaphoreType.DMA((n_copies,)),
            *tile_scratch(weight, tile_of(width, 512), transposed),
        ],
        out_shape=[jax.ShapeDtypeStruct((rows, width), jnp.bfloat16) for rows in out_rows],
        compiler_params=pltpu.CompilerParams(vmem_limit_bytes=18 * MIB),
        cost_estimate=NO_COST,
    )(me, *sources, pltpu.with_memory_space_constraint(weight, pltpu.HBM))


def project(me, chips, rows, slots, weight, transposed):
    total = sum(s.shape[0] for s in slots)
    height = slots[0].shape[0]
    piece = min(rows, height)

    def place(me, slots, held):
        places = []
        for first in range(0, total, piece):
            part, within = divmod(first, rows)
            core = jnp.bitwise_xor(lax.rem(me, CORES), part % CORES)
            chip = jnp.bitwise_xor(lax.div(me, CORES), part // CORES)
            at = pl.multiple_of((core * chips + chip) * rows + within, piece)
            source = slots[first // height].at[pl.ds(first % height, piece)]
            places.append((source, held.at[pl.ds(at, piece)]))
        return places

    cut = total // CORES
    out_rows = [cut] * CORES
    copies = total // piece
    return product_call(me, place, slots, copies, weight, transposed, out_rows)


def expand(me, chips, rows, parts, n_slots, weight, transposed):
    def place(me, parts, held):
        return gathered_places(me, chips, rows, parts, held)

    out_rows = [CORES * chips * rows // n_slots] * n_slots
    return product_call(me, place, parts, len(parts), weight, transposed, out_rows)


def weight_kernel(rows, chips, parts_left, n_slots, n_parts, tile, first, me, *refs):
    slots, parts = refs[:n_slots], refs[n_slots : n_slots + n_parts]
    out, held_slots, held_parts, sems = refs[-4:]
    step = pl.program_id(0) + first

    @pl.when(pl.program_id(0) == 0)
    def _():
        places = slot_places(slots, held_slots)
        places += gathered_places(me[0], chips, rows, parts, held_parts)
        copies = copies_of(places, sems)
        start_all(copies)
        finish_all(copies)

    left, right = (held_parts, held_slots) if parts_left else (held_slots, held_parts)
    columns = left[:, pl.ds(pl.multiple_of(step * tile, tile), tile)]
    out[...] = narrow(product(columns, right[...], ((0,), (0,))))


def weight_product(me, rows, chips, slots, parts, parts_left, span=(0, 1), into=()):
    total = sum(s.shape[0] for s in slots)
    slot_width, part_width = slots[0].shape[1], parts[0].shape[1]
    tall, width = (part_width, slot_width) if parts_left else (slot_width, part_width)
    tile = tile_of(tall, 512)
    share, shares = span
    first, last = (tall // tile * at // shares for at in (share, share + 1))
    n_in = len(slots) + len(parts) + len(into)
    return pl.pallas_call(
        functools.partial(
            weight_kernel, rows, chips, parts_left, len(slots), len(parts), tile, first
        ),
        grid_spec=pltpu.PrefetchScalarGridSpec(
            num_scalar_prefetch=1,
            grid=(last - first,),
            in_specs=[HERE] * n_in,
            out_specs=pl.BlockSpec((tile, width), lambda j, me: (j + first, 0)),
            scratch_shapes=[
                pltpu.VMEM((total, slot_width), jnp.bfloat16),
                pltpu.VMEM((total, part_width), jnp.bfloat16),
                pltpu.SemaphoreType.DMA((len(slots) + len(parts),)),
            ],
        ),
        out_shape=jax.ShapeDtypeStruct((tall, width), jnp.bfloat16),
        input_output_aliases={n_in: 0} if into else {},
        compiler_params=pltpu.CompilerParams(vmem_limit_bytes=40 * MIB),
        cost_estimate=NO_COST,
    )(me, *slots, *parts, *into)


class Program:
    def __init__(self, token):
        self.token = token

    def placed(self, values):
        return lax.optimization_barrier((*values, self.token))[:-1]

    def passed(self, values):
        *values, self.token = lax.optimization_barrier((*values, self.token))
        return values

    def start(self, value, axis, pairs):
        (value,) = self.placed([value])
        return lax.ppermute(value, axis, pairs)

    def wait(self, moving):
        return self.passed([moving])[0]

    def compute(self, step, *values):
        leaves, tree = jax.tree.flatten(step(*self.placed(values)))
        return jax.tree.unflatten(tree, self.passed(leaves))


def shards(sizes, tokens, w_in, w_out, spike_gain, cotangent):
    n_row, n_col, n_dp = sizes["row"], sizes["col"], sizes["dp"]
    chips = n_col // CORES
    chunks = CHUNKS if n_row % CHUNKS == 0 else 1
    per = n_row // chunks
    part = per * tokens.shape[0] // n_col
    me = lax.axis_index("col").astype(jnp.int32).reshape(1)
    run = Program(me)

    def row_start(value, by=1):
        return run.start(value, "row", [(i, (i + by) % n_row) for i in range(n_row)])

    def core_start(value):
        return run.start(value, "col", [(i, i ^ 1) for i in range(n_col)])

    def chip_start(values):
        return [
            run.start(value, "col", [(i, i ^ (CORES * k)) for i in range(n_col)])
            for k, value in zip(range(1, chips), values)
        ]

    def half_start(value):
        return [
            run.start(value, "dp", [(d, (d + k) % n_dp) for d in range(n_dp)])
            for k in range(1, n_dp)
        ]

    def wait_all(moving):
        return [run.wait(value) for value in moving]

    def in_one_step(step):
        def taken(*values):
            def otherwise(*values):
                made = jax.eval_shape(step, *values)
                return jax.tree.map(lambda v: jnp.zeros(v.shape, v.dtype), made)

            return lax.cond(me[0] < n_col, step, otherwise, *values)

        taken.__name__ = step.__name__
        return taken

    def swap(value):
        return lax.ppermute(value, "col", [(i, i ^ 1) for i in range(n_col)])

    def part_sum(own, theirs, k):
        rows = slice(k * part, (k + 1) * part)
        return wide(own[rows]) + wide(theirs[rows])

    def forward(*slots):
        return project(me, chips, part, slots, w_in, False)

    def backward(*slots):
        return project(me, chips, part, slots, w_out, True)

    @in_one_step
    def chip_sums(own, for_sibling):
        theirs = swap(for_sibling)
        return [theirs] + [narrow(part_sum(own, theirs, k)) for k in range(1, chips)]

    def projected(step, slots):
        own, for_sibling = run.compute(step, *slots)
        return [own] + run.compute(chip_sums, own, for_sibling)

    @in_one_step
    def both_cores_now(*mine):
        return [swap(value) for value in mine]

    def expand_out(*parts):
        return expand(me, chips, part, parts, per, w_out, False)

    def expand_back(*parts):
        return expand(me, chips, part, parts, per, w_in, True)

    def spread_out(step, mine):
        parts = [*mine] + run.compute(both_cores_now, *mine)
        return run.compute(step, *parts), parts

    def whole(own, theirs, arrived):
        total = part_sum(own, theirs, 0)
        for value in arrived:
            total = total + wide(value)
        return total

    def fire(own, theirs, *arrived):
        total, slope = spike_parts(whole(own, theirs, arrived), spike_gain)
        return narrow(total), slope

    def slope_back(slope, own, theirs, *arrived):
        return narrow(whole(own, theirs, arrived) * slope)

    def ring_add(arrived, slot):
        return narrow(wide(arrived) + wide(slot))

    def weight_step(parts_left, share, shares):
        n_into = 1 if share > 0 else 0

        def weights(*values):
            into, values = values[:n_into], values[n_into:]
            slots, parts = values[:n_all], values[n_all:]
            span = (share, shares)
            return weight_product(me, part, chips, slots, parts, parts_left, span, into)

        return weights

    n_all = n_row * n_dp
    tok, cot, outs, back, summed = [], [], [], [], []

    def row_lane():
        for own, slots in ((tokens, tok), (cotangent, cot)):
            slots.append(own)
            ahead, behind = own, own
            low, high, late = 1, n_row, []
            while low < high:
                both = low > 1 and high - low > 1
                moving = [row_start(ahead)] + ([row_start(behind, -1)] if both else [])
                yield
                ahead, *rest = [run.wait(value) for value in moving]
                slots.append(ahead)
                low += 1
                if both:
                    (behind,) = rest
                    late.insert(0, behind)
                    high -= 1
            slots.extend(late)
        for slots in (outs, back):
            held = slots[1 % n_row]
            for s in range(2, n_row + 1):
                moving = row_start(held)
                yield
                held = run.compute(ring_add, run.wait(moving), slots[s % n_row])
            summed.append(held)

    row = row_lane()

    def turn():
        next(row, None)

    def until(slots, count):
        while len(slots) < count:
            turn()

    first, second = list(range(per)), list(range(per, n_row))
    far = {}
    spikes, slopes, grads = [], [], []
    sources = {"tok": tok, "cot": cot, "spike": spikes, "grad": grads}

    def half_lane():
        queue = [[("tok", 0), ("cot", 0)]] + [[("tok", s)] for s in first[1:]]
        queue += [[("spike", 0)]] + [[("tok", s)] for s in second[:-1]]
        queue += [[("spike", c)] for c in range(1, chunks)]
        queue += [[("cot", s)] for s in first[1:]] + [[("grad", 0)]]
        queue += [[("cot", s)] for s in second]
        queue += [[("grad", c)] for c in range(1, chunks)]
        queue += [[("tok", s)] for s in second[-1:]]
        for group in queue:
            moving = [
                half_start(cotangent if (kind, at) == ("cot", 0) else sources[kind][at])
                for kind, at in group
            ]
            yield
            for place, values in zip(group, moving):
                far[place] = wait_all(values)

    half = half_lane()

    def half_turn():
        next(half, None)

    def spreading(value):
        return value, chip_start([value] * (chips - 1))

    def both_cores(mine):
        return [core_start(value) for value in mine]

    def chunk(slots, c):
        return slots[c * per : (c + 1) * per]

    turn()
    half_turn()
    until(tok, per)
    own, theirs, *sums = projected(forward, chunk(tok, 0))
    moving = chip_start(sums)
    half_turn()
    until(tok, n_row - 1)
    spike, slope = run.compute(fire, own, theirs, *wait_all(moving))
    spikes.append(spike)
    slopes.append(slope)
    gather = spreading(spike)
    half_turn()
    until(tok, n_row)

    grad_partials, grad_sums, mine, spike_all = [], [], [], []

    def project_back(c):
        until(cot, (c + 1) * per)
        own, theirs, *sums = projected(backward, chunk(cot, c))
        grad_partials.append((own, theirs))
        grad_sums.append(sums)

    def expanded(c):
        slots, parts = spread_out(expand_out, mine[c])
        outs.extend(slots)
        spike_all.extend(parts)

    for c in range(1, chunks):
        own, theirs, *sums = projected(forward, chunk(tok, c))
        mine.append([gather[0]] + wait_all(gather[1]))
        moving = chip_start(sums)
        half_turn()
        if c + 1 == chunks:
            project_back(0)
        spike, slope = run.compute(fire, own, theirs, *wait_all(moving))
        spikes.append(spike)
        slopes.append(slope)
        gather = spreading(spike)
        half_turn()
        expanded(c - 1)
        half_turn()
    if chunks == 1:
        project_back(0)
    until(cot, n_row - 1)
    mine.append([gather[0]] + wait_all(gather[1]))
    grad_moving = chip_start(grad_sums[0])
    expanded(chunks - 1)
    until(cot, n_row)

    grad_all = []
    for c in range(chunks):
        grad = run.compute(
            slope_back, slopes[c], *grad_partials[c], *wait_all(grad_moving)
        )
        grads.append(grad)
        gather = spreading(grad)
        if c + 1 < chunks:
            half_turn()
            project_back(c + 1)
        else:
            turn()
        grad_mine = [gather[0]] + wait_all(gather[1])
        if c + 1 < chunks:
            grad_moving = chip_start(grad_sums[c + 1])
            turn()
        else:
            far_moving = chip_start(far["spike", 0][:1] * (chips - 1))
        if c + 1 < chunks:
            half_turn()
        slots, parts = spread_out(expand_back, grad_mine)
        back.extend(slots)
        grad_all.extend(parts)
        half_turn()

    todo = [
        (kind, c, h)
        for kind in ("spike", "grad")
        for h in range(n_dp - 1)
        for c in range(chunks)
    ]
    spread = {"spike": [], "grad": []}
    waiting = None

    def settle():
        if waiting is not None:
            kind, held, others = waiting
            spread[kind].extend(held + wait_all(others))

    def every(kind, slots):
        return slots + [far[kind, s][h] for h in range(n_dp - 1) for s in range(n_row)]

    def gradient(parts_left, share, shares, *into):
        kind, slots, parts = (
            ("spike", every("cot", cot), spike_all)
            if parts_left
            else ("grad", every("tok", tok), grad_all)
        )
        step = weight_step(parts_left, share, shares)
        return run.compute(step, *into, *slots, *parts, *spread[kind])

    spikes_last = len(todo) // 2 - 1
    weight_out = None
    for i, (kind, c, h) in enumerate(todo):
        held = [far[kind, c][h]] + wait_all(far_moving)
        others = both_cores(held)
        if i + 1 < len(todo):
            kind_next, c_next, h_next = todo[i + 1]
            while (kind_next, c_next) not in far:
                half_turn()
            far_moving = chip_start([far[kind_next, c_next][h_next]] * (chips - 1))
        settle()
        waiting = (kind, held, others)
        if i < spikes_last:
            turn()
            half_turn()
        elif i == spikes_last:
            settle()
            waiting = None
            while ("cot", n_row - 1) not in far:
                half_turn()
            weight_out = gradient(True, 0, 2)
            half_turn()
        elif i == spikes_last + 1:
            turn()
            weight_out = gradient(True, 1, 2, weight_out)
        else:
            turn()
    settle()
    while ("tok", n_row - 1) not in far:
        half_turn()
    weight_in = gradient(False, 0, 1)
    while len(summed) < 2:
        turn()
    return (summed[0], summed[1], weight_in, weight_out)


def solution(mesh):
    placed = (
        P(("dp", "row"), "col"),
        P("col", "row"),
        P("row", "col"),
        P("row"),
        P(("dp", "row"), "col"),
    )

    def program(*args):
        return shards(mesh.shape, *args)

    return jax.shard_map(
        program,
        mesh=mesh,
        in_specs=placed,
        out_specs=(
            P(("dp", "row"), "col"),
            P(("dp", "row"), "col"),
            P("col", "row"),
            P("row", "col"),
        ),
        check_vma=False,
    )
```
